32 devices in a mesh: groups: 2 (over x), replica: 8 (over z, y), tensor: 2 (over core).
Axes of the slice: x: 2, y: 2, z: 4, core: 2. Of those that a mesh axis runs over, the one named last changes fastest.
Arguments:
- tokens: bfloat16 [2048, 5120], P(('groups', 'replica'), 'tensor'), parts along dimension 0, may hold values from -6 to 6
- cotangent: bfloat16 [2048, 512], P(('groups', 'replica'), 'tensor'), parts along dimension 0, may hold values from -6 to 6
- key_weight: bfloat16 [512, 5120], P('tensor'), may hold values from -0.078125 to 0.078125
- momentum: bfloat16 [16, 512, 5120], P(('groups', 'replica'), 'tensor'), parts along dimension 0, may hold values from -60 to 60
- indices: int32 [8, 80, 8], P('tensor'), may hold values from 0 to 4095, as said below
Outputs:
- keys: bfloat16 [2048, 512], P(('groups', 'replica'), 'tensor'), parts along dimension 0
- input_grad: bfloat16 [2048, 5120], P(('groups', 'replica'), 'tensor'), parts along dimension 0
- new_momentum: bfloat16 [16, 512, 5120], P(('groups', 'replica'), 'tensor'), parts along dimension 0
- update: bfloat16 [1024, 5120], P(('groups', 'tensor')), parts along dimension 0
- pooled: float32 [16, 80, 8], P(('groups', 'tensor')), parts along dimension 0
The draws below stay inside these ranges and needn't reach their ends.
There are 2 independent parts, one for each index of `groups`. The reference program is written for one: setup_inputs(seed, part) draws one part's arguments, and reference() takes and returns one part's arrays. A program takes and returns all parts, laid end to end along the dimension named above; an argument that names none is the same for every part. Nothing has to cross between parts.
Inputs may be any that keep to these rules, and one draw needn't show every extreme that they name: `indices`: within a span the 8 positions are distinct.
All inputs are finite; a program needn't handle non-finite values.
Results may differ from the reference program's by a relative error of at most 0.001.
Values may be sent and summed in bfloat16 or wider, within the bound.
No kernel may reach another device: no remote copies, remote signals or barrier semaphores. Data moves between devices by JAX's collectives and lax.ppermute only.
A program may use at most 128 MiB of HBM per device.

```python
import jax
import jax.numpy as jnp
from jax import lax

D = 5120
KVW = 512
SPAN = 64
KEEP = 8
TOK_DEV = 128
REPLICAS = 8
TOKENS = 1024


def draw_momentum(key, part):
    key = jax.random.fold_in(key, 11)
    first = jax.random.fold_in(key, 0)
    base = jnp.clip(jax.random.normal(first, (REPLICAS, KVW, D), jnp.float32), -6.0, 6.0)
    ramp = 1.0 + 2.0 * jnp.arange(REPLICAS, dtype=jnp.float32) / max(REPLICAS - 1, 1)
    field = base
    return jnp.clip(3.0 * field * ramp[:, None, None], -60.0, 60.0).astype(jnp.bfloat16)


def draw_indices(key, part):
    key = jax.random.fold_in(key, 23)
    shape = (KVW // SPAN, D // SPAN, SPAN * SPAN)
    scores = jax.random.randint(key, shape, 0, 2 ** 17, jnp.int32) * (SPAN * SPAN)
    scores = scores + jnp.arange(SPAN * SPAN, dtype=jnp.int32)
    scores = scores.at[0, 0, 0].add(2 ** 29)
    scores = scores.at[0, 0, SPAN * SPAN - 1].add(2 ** 29)
    picked = jax.lax.top_k(scores, KEEP)[1]
    return picked.astype(jnp.int32)


def shard_levels(stream_key, dims, cuts, least, high):
    level = 1.0
    for axis_at, parts in cuts:
        draws = jax.random.uniform(jax.random.fold_in(jax.random.fold_in(stream_key, 6), axis_at), (parts,), jnp.float32, least / len(cuts), high / len(cuts))
        level = level * jnp.repeat(jnp.exp(draws), dims[axis_at] // parts).reshape((-1,) + (1,) * (len(dims) - 1 - axis_at))
    return level


def noise(key, shape, scale, reach, cuts=(), kind=jnp.bfloat16):
    drawn = scale * jax.random.normal(key, shape, jnp.float32)
    if cuts:
        drawn = drawn * shard_levels(key, shape, cuts, -0.22, 0.18)
    return jnp.clip(drawn, -reach, reach).astype(kind)


def setup_inputs(seed: int = 0, part: int = 0) -> dict:
    keys = jax.random.split(jax.random.key(seed), 6)
    part_splits = jax.random.split(jax.random.fold_in(keys[5], part), 6)
    tokens = noise(part_splits[0], (TOKENS, D), 1.0, 6.0, ((0, 8), (1, 2)))
    cotangent = noise(part_splits[1], (TOKENS, KVW), 1.0, 6.0, ((0, 8), (1, 2)))
    key_weight = noise(keys[2], (KVW, D), D ** -0.5, 0.078125, ((0, 2),))
    momentum = draw_momentum(jax.random.fold_in(jax.random.fold_in(keys[5], part), 71), part)
    indices = draw_indices(jax.random.fold_in(keys[5], 71), part)
    return dict(tokens=tokens, cotangent=cotangent, key_weight=key_weight, momentum=momentum, indices=indices)


decay_rate = 0.9

def dct_table(order):
    freq = jnp.arange(order, dtype=jnp.float32)[:, None]
    place = jnp.arange(order, dtype=jnp.float32)[None, :]
    scale = jnp.where(freq == 0, jnp.sqrt(1.0 / order), jnp.sqrt(2.0 / order))
    return (scale * jnp.cos(jnp.pi * (2.0 * place + 1.0) * freq / (2.0 * order))).astype(jnp.float32)

def table_rows(indices, table):
    first = jnp.take(table, (indices // SPAN).astype(jnp.int32), axis=0)
    second = jnp.take(table, (indices % SPAN).astype(jnp.int32), axis=0)
    return (first, second)

def select_coefs(field, indices, table):
    rows, cols = field.shape
    blocks = field.reshape(rows // SPAN, SPAN, cols // SPAN, SPAN)
    first, second = table_rows(indices, table)
    partial_rows = jnp.einsum('ijta,iajb->ijtb', first, blocks, precision=lax.Precision.HIGHEST)
    return lax.optimization_barrier(jnp.sum(partial_rows * second, axis=3))

def decode(coefs, indices, table):
    first, second = table_rows(indices, table)
    blocks = jnp.einsum('ijta,ijt,ijtb->iajb', first, coefs, second, precision=lax.Precision.HIGHEST)
    nrow, side, ncol, other = blocks.shape
    return blocks.reshape(nrow * side, ncol * other)

def reference(tokens, cotangent, key_weight, momentum, indices):
    table = dct_table(SPAN)
    tok_blocks = tokens.reshape(REPLICAS, TOK_DEV, D)
    cot_blocks = cotangent.reshape(REPLICAS, TOK_DEV, KVW)

    def one_replica(inputs):
        source, grad_out, state = inputs
        key_rows = jnp.dot(source, key_weight.T, preferred_element_type=jnp.float32).astype(jnp.bfloat16)
        in_rows = jnp.dot(grad_out, key_weight, preferred_element_type=jnp.float32).astype(jnp.bfloat16)
        grad = jnp.dot(grad_out.T, source, preferred_element_type=jnp.float32)
        moved = decay_rate * state.astype(jnp.float32) + grad
        coefs = select_coefs(moved, indices, table)
        remain = (moved - decode(coefs, indices, table)).astype(jnp.bfloat16)
        return (key_rows, in_rows, remain, coefs)
    outs, ins, remains, all_coefs = lax.map(one_replica, (tok_blocks, cot_blocks, momentum))
    pooled = lax.optimization_barrier(jnp.sum(all_coefs, axis=0)) / REPLICAS
    update = decode(pooled, indices, table).astype(jnp.bfloat16)
    return (outs.reshape(TOKENS, KVW), ins.reshape(TOKENS, D), remains, update, pooled)
```

```python
import functools

import jax
import jax.numpy as jnp
import numpy as np
from jax import lax
from jax.experimental import pallas as pl
from jax.experimental.pallas import tpu as pltpu
from jax.sharding import PartitionSpec as P

SPAN = 64
GROUP = 4
SIDE = SPAN * GROUP
decay_rate = 0.9
bf16 = jnp.bfloat16
f32 = jnp.float32
VMEM = pltpu.VMEM


def split(x):
    hi = x.astype(bf16)
    return hi, (x - hi.astype(f32)).astype(bf16)


def tables():
    freq = np.arange(SPAN, dtype=np.float64)[:, None]
    place = np.arange(SPAN, dtype=np.float64)[None, :]
    scale = np.where(freq == 0, np.sqrt(1.0 / SPAN), np.sqrt(2.0 / SPAN))
    table = scale * np.cos(np.pi * (2.0 * place + 1.0) * freq / (2.0 * SPAN))
    block = np.kron(np.eye(GROUP), table)

    def parts(x):
        x = x.astype(np.float32)
        hi = x.astype(jnp.bfloat16)
        return hi, (x - hi.astype(np.float32)).astype(jnp.bfloat16)

    decayed = np.concatenate(parts(np.float32(decay_rate).astype(np.float64) * block), axis=1)
    plain = np.concatenate(parts(block), axis=1)
    back = np.concatenate(parts(block.T), axis=0)
    return decayed, plain, back


def mm(a, b):
    return jnp.dot(a, b, preferred_element_type=f32)


def mm_t(a, b):
    return lax.dot_general(a, b, (((1,), (1,)), ((), ())), preferred_element_type=f32)


def params(mib=16):
    return pltpu.CompilerParams(vmem_limit_bytes=mib * 2**20)


def vmem(x):
    return pltpu.with_memory_space_constraint(x, VMEM)


def whole(n):
    return [pl.BlockSpec(memory_space=VMEM)] * n


def plan_kernel(idx_ref, g_ref, decayed_ref, plain_ref, back_ref, sel_ref, selg_ref, lt_ref, sec_ref, gt_ref, tmp):
    blocks, kept = idx_ref.shape
    keep = kept // (GROUP * GROUP)
    tmp[...] = jnp.zeros(tmp.shape, jnp.int32)
    tmp[0:blocks, :] = idx_ref[...]
    idx = tmp[...]
    lane = lax.broadcasted_iota(jnp.int32, idx.shape, 1)
    a_row = (idx >> 6) + SPAN * (lane // (GROUP * keep))
    b_row = (idx & (SPAN - 1)) + SPAN * ((lane // keep) & (GROUP - 1))
    a_col, b_col = a_row.T, b_row.T
    gt = g_ref[...].astype(f32).T.astype(bf16)
    gt_ref[...] = gt
    plain = plain_ref[...]
    row_g = mm_t(plain[:, :SIDE], gt.T) + mm_t(plain[:, SIDE:], gt.T)
    row_hi, row_lo = split(row_g)
    row_tab = jnp.concatenate([decayed_ref[...], row_hi, row_lo], axis=1)
    lanes = lax.broadcasted_iota(jnp.int32, (kept, SIDE), 1)
    subs = lax.broadcasted_iota(jnp.int32, (SIDE, kept), 0)
    for j in range(blocks):
        one_a = jnp.where(lanes == a_col[:, j : j + 1], 1.0, 0.0).astype(bf16)
        one_b = jnp.where(lanes == b_col[:, j : j + 1], 1.0, 0.0).astype(bf16)
        one_t = jnp.where(subs == a_row[j : j + 1, :], 1.0, 0.0).astype(bf16)
        rows = mm(one_a, row_tab)
        sel_ref[j, 0:kept, :] = rows[:, :SIDE].astype(bf16)
        sel_ref[j, kept:, :] = rows[:, SIDE : 2 * SIDE].astype(bf16)
        tok = row_g.shape[1]
        selg_ref[j, 0:kept, :] = rows[:, 2 * SIDE : 2 * SIDE + tok].astype(bf16)
        selg_ref[j, kept:, :] = rows[:, 2 * SIDE + tok :].astype(bf16)
        cols = mm(one_b, plain)
        sec_ref[j] = cols[:, :SIDE] + cols[:, SIDE:]
        rev = mm(back_ref[...], one_t)
        lt_ref[j, :, 0:kept] = rev[:SIDE].astype(bf16)
        lt_ref[j, :, kept:] = rev[SIDE:].astype(bf16)


def plan(idx, g, tabs):
    blocks, kept = idx.shape
    tok, rows = g.shape
    return pl.pallas_call(
        plan_kernel,
        in_specs=whole(5),
        out_specs=whole(5),
        out_shape=[
            VMEM((blocks, 2 * kept, SIDE), bf16),
            VMEM((blocks, 2 * kept, tok), bf16),
            VMEM((blocks, SIDE, 2 * kept), bf16),
            VMEM((blocks, kept, SIDE), f32),
            VMEM((rows, tok), bf16),
        ],
        scratch_shapes=[pltpu.VMEM((kept, kept), jnp.int32)],
        compiler_params=params(),
        name="plan",
    )(idx, g, *tabs)


def pick(t_ref, own_ref, peer_ref, j, half):
    h, at = divmod(j, half)
    cols = slice(at * SIDE, (at + 1) * SIDE)
    return jnp.where(t_ref[0] == h, own_ref[:, cols], peer_ref[:, cols])


def select_kernel(t_ref, sel_ref, selg_ref, sec_ref, m_ref, own_ref, peer_ref, row_ref, col_ref):
    blocks, kept = sel_ref.shape[0], sel_ref.shape[1] // 2
    half = blocks // 2
    lane = lax.broadcasted_iota(jnp.int32, (kept, kept), 1)
    acc = jnp.zeros((kept, kept), f32)
    for j in range(blocks):
        x = pick(t_ref, own_ref, peer_ref, j, half)
        m = m_ref[:, j * SIDE : (j + 1) * SIDE]
        r = mm(sel_ref[j], m) + mm(selg_ref[j], x)
        r = (r[:kept] + r[kept:]) * sec_ref[j]
        acc = jnp.where(lane == j, jnp.sum(r, axis=1, keepdims=True), acc)
    col_ref[...] = acc
    row_ref[...] = acc.T[:blocks]


def select(t, sel, selg, sec, m, own, peer):
    blocks, kept = sel.shape[0], sel.shape[1] // 2
    return pl.pallas_call(
        select_kernel,
        in_specs=[pl.BlockSpec(memory_space=pltpu.SMEM)] + whole(6),
        out_specs=whole(2),
        out_shape=[VMEM((blocks, kept), f32), VMEM((kept, kept), f32)],
        compiler_params=params(),
        name="select",
    )(t, vmem(sel), vmem(selg), vmem(sec), vmem(m), vmem(own), vmem(peer))


def spread(lt, sec, c):
    hi, lo = split(sec * c)
    kept = hi.shape[0]
    return mm(lt, jnp.concatenate([hi, hi], axis=0)) + mm(lt[:, :kept], lo)


CHUNKS = 4


def remain_kernel(t_ref, lt_ref, sec_ref, gt_ref, m_ref, own_ref, peer_ref, col_ref, out_ref, buf, sems):
    blocks = lt_ref.shape[0]
    per = blocks // CHUNKS
    copies = []
    for j in range(blocks):
        x = pick(t_ref, own_ref, peer_ref, j, blocks // 2)
        cols = slice(j * SIDE, (j + 1) * SIDE)
        lt = lt_ref[j]
        kept = lt.shape[1] // 2
        hi, lo = split(sec_ref[j] * -col_ref[:, j : j + 1])
        moved = decay_rate * m_ref[:, cols].astype(f32)
        moved += mm(jnp.concatenate([lt[:, :kept], gt_ref[...]], axis=1), jnp.concatenate([lo, x], axis=0))
        moved += mm(lt, jnp.concatenate([hi, hi], axis=0))
        buf[:, cols] = moved.astype(bf16)
        if (j + 1) % per == 0:
            at = pl.ds((j + 1 - per) * SIDE, per * SIDE)
            copies.append(pltpu.make_async_copy(buf.at[:, at], out_ref.at[:, at], sems.at[j // per]))
            copies[-1].start()
    for copy in copies:
        copy.wait()


def remain(t, lt, sec, gt, m, own, peer, col):
    return pl.pallas_call(
        remain_kernel,
        in_specs=[pl.BlockSpec(memory_space=pltpu.SMEM)] + whole(7),
        out_specs=pl.BlockSpec(memory_space=pl.ANY),
        out_shape=jax.ShapeDtypeStruct(m.shape, bf16),
        scratch_shapes=[pltpu.VMEM(m.shape, bf16), pltpu.SemaphoreType.DMA((CHUNKS,))],
        compiler_params=params(),
        name="remain",
    )(t, vmem(lt), vmem(sec), vmem(gt), vmem(m), vmem(own), vmem(peer), vmem(col))


def update_kernel(scale, lt_ref, sec_ref, sum_ref, out_ref, mean_ref, buf, tmp, sems):
    blocks, kept = sum_ref.shape
    per = blocks // CHUNKS
    mean = sum_ref[...] * scale
    mean_ref[...] = mean
    tmp[...] = jnp.zeros(tmp.shape, f32)
    tmp[0:blocks, :] = mean
    col = tmp[...].T
    copies = []
    for j in range(blocks):
        cols = slice(j * SIDE, (j + 1) * SIDE)
        buf[:, cols] = spread(lt_ref[j], sec_ref[j], col[:, j : j + 1]).astype(bf16)
        if (j + 1) % per == 0:
            at = pl.ds((j + 1 - per) * SIDE, per * SIDE)
            copies.append(pltpu.make_async_copy(buf.at[:, at], out_ref.at[:, at], sems.at[j // per]))
            copies[-1].start()
    for copy in copies:
        copy.wait()


def update(lt, sec, total, replicas, shape):
    blocks, kept = total.shape
    return pl.pallas_call(
        functools.partial(update_kernel, 1.0 / replicas),
        in_specs=whole(3),
        out_specs=[pl.BlockSpec(memory_space=pl.ANY)] + whole(1),
        out_shape=[jax.ShapeDtypeStruct(shape, bf16), jax.ShapeDtypeStruct(total.shape, f32)],
        scratch_shapes=[
            pltpu.VMEM(shape, bf16),
            pltpu.VMEM((kept, kept), f32),
            pltpu.SemaphoreType.DMA((CHUNKS,)),
        ],
        compiler_params=params(),
        name="update",
    )(vmem(lt), vmem(sec), vmem(total))


def keys_kernel(t_ref, own_ref, peer_ref, w_ref, out_ref):
    width = own_ref.shape[1]
    t = t_ref[0]
    mine = pl.ds(pl.multiple_of(t * width, width), width)
    theirs = pl.ds(pl.multiple_of((1 - t) * width, width), width)
    out_ref[...] = (mm_t(own_ref[...], w_ref[:, mine]) + mm_t(peer_ref[...], w_ref[:, theirs])).astype(bf16)


def keys_of(t, own, peer, w):
    return pl.pallas_call(
        keys_kernel,
        in_specs=[pl.BlockSpec(memory_space=pltpu.SMEM)] + whole(3),
        out_specs=pl.BlockSpec(memory_space=VMEM),
        out_shape=jax.ShapeDtypeStruct((own.shape[0], w.shape[0]), bf16),
        compiler_params=params(),
        name="keys",
    )(t, vmem(own), vmem(peer), vmem(w))


def input_kernel(t_ref, own_ref, peer_ref, w_ref, wp_ref, out_ref):
    width = out_ref.shape[1]
    at = pl.ds(pl.multiple_of(t_ref[0] * width, width), width)
    out_ref[...] = (mm(own_ref[...], w_ref[:, at]) + mm(peer_ref[...], wp_ref[:, at])).astype(bf16)


def input_of(t, own, peer, w, wp):
    return pl.pallas_call(
        input_kernel,
        in_specs=[pl.BlockSpec(memory_space=pltpu.SMEM)] + whole(4),
        out_specs=pl.BlockSpec(memory_space=VMEM),
        out_shape=jax.ShapeDtypeStruct((own.shape[0], w.shape[1] // 2), bf16),
        compiler_params=params(),
        name="input_grad",
    )(t, vmem(own), vmem(peer), vmem(w), vmem(wp))


def replica_sum(x, n):
    if n & (n - 1):
        return lax.psum(x, "replica")
    step = 1
    while step < n:
        x = x + lax.ppermute(x, "replica", [(i, i ^ step) for i in range(n)])
        step *= 2
    return x


def shards(tokens, cotangent, key_weight, momentum, indices):
    replicas = lax.axis_size("replica")
    swap = [(0, 1), (1, 0)]
    t = lax.axis_index("tensor").astype(jnp.int32).reshape(1)
    peer = lax.ppermute(tokens, "tensor", swap)
    cot_peer = lax.ppermute(cotangent, "tensor", swap)
    w_peer = lax.ppermute(key_weight, "tensor", swap)
    m = momentum[0]
    nrow, ncol, keep = indices.shape
    blocks = ncol // GROUP
    idx = indices.reshape(nrow, blocks, GROUP, keep).transpose(1, 0, 2, 3).reshape(blocks, nrow * GROUP * keep)
    sel, selg, lt, sec, gt = plan(idx, cotangent, tables())
    row, col = select(t, sel, selg, sec, m, tokens, peer)
    total = replica_sum(row, replicas)
    remaining = remain(t, lt, sec, gt, m, tokens, peer, col)
    keys = keys_of(t, tokens, peer, key_weight)
    input_grad = input_of(t, cotangent, cot_peer, key_weight, w_peer)
    new_update, mean = update(lt, sec, total, replicas, m.shape)
    pooled = mean.reshape(blocks, nrow, GROUP, keep).transpose(1, 0, 2, 3).reshape(nrow, ncol, keep)
    return (keys, input_grad, remaining[None], new_update, pooled)


def solution(mesh):
    placed = (
        P(("groups", "replica"), "tensor"),
        P(("groups", "replica"), "tensor"),
        P("tensor", None),
        P(("groups", "replica"), "tensor", None),
        P("tensor", None, None),
    )
    return jax.shard_map(
        shards,
        mesh=mesh,
        in_specs=placed,
        out_specs=(
            P(("groups", "replica"), "tensor"),
            P(("groups", "replica"), "tensor"),
            P(("groups", "replica"), "tensor", None),
            P(("groups", "tensor"), None),
            P(("groups", "tensor"), None, None),
        ),
        check_vma=False,
    )
```

```python
import functools

import jax
import jax.numpy as jnp
import numpy as np
from jax import lax
from jax.experimental import pallas as pl
from jax.experimental.pallas import tpu as pltpu
from jax.sharding import PartitionSpec as P

SPAN = 64
GROUP = 4
SIDE = SPAN * GROUP
LANES = 128
ROWS = 16
decay_rate = 0.9
bf16 = jnp.bfloat16
f32 = jnp.float32
VMEM = pltpu.VMEM


def split(x):
    hi = x.astype(bf16)
    return hi, (x - hi.astype(f32)).astype(bf16)


def block_table():
    freq = np.arange(SPAN, dtype=np.float64)[:, None]
    place = np.arange(SPAN, dtype=np.float64)[None, :]
    scale = np.where(freq == 0, np.sqrt(1.0 / SPAN), np.sqrt(2.0 / SPAN))
    table = scale * np.cos(np.pi * (2.0 * place + 1.0) * freq / (2.0 * SPAN))
    return np.kron(np.eye(GROUP), table).astype(np.float32)


def mm(a, b):
    return jnp.dot(a, b, preferred_element_type=f32)


def mm_t(a, b):
    return lax.dot_general(a, b, (((1,), (1,)), ((), ())), preferred_element_type=f32)


def call(kernel, name, flops=0, nbytes=0, **kw):
    return pl.pallas_call(
        kernel,
        name=name,
        compiler_params=pltpu.CompilerParams(vmem_limit_bytes=8 * 2**20),
        cost_estimate=pl.CostEstimate(flops=flops, bytes_accessed=nbytes, transcendentals=0),
        **kw,
    )


def vmem(*xs):
    return [pltpu.with_memory_space_constraint(x, VMEM) for x in xs]


def hbm(*xs):
    return [pltpu.with_memory_space_constraint(x, pltpu.HBM) for x in xs]


def whole(n):
    return [pl.BlockSpec(memory_space=VMEM)] * n


def anywhere(n):
    return [pl.BlockSpec(memory_space=pl.ANY)] * n


SCALAR = pl.BlockSpec(memory_space=pltpu.SMEM)


def column(z, j):
    keep = z.shape[0] // GROUP
    parts = [
        jnp.broadcast_to(z[i * keep : (i + 1) * keep, c : c + 1], (keep, LANES))
        for i in range(GROUP)
        for c in range(j * GROUP, (j + 1) * GROUP)
    ]
    return jnp.concatenate(parts, axis=0)


def flat(ref):
    nrow, keep, ncol = ref.shape
    return ref[...].reshape(nrow * keep, ncol)


def plan_kernel(idx_ref, g_ref, tab_ref, m_hbm, x_hbm, sel_ref, sec_ref, lt_ref, gt_ref, m_ref, x_ref, sems):
    loads = [
        pltpu.make_async_copy(src, dst, sems.at[n])
        for n, (src, dst) in enumerate(((x_hbm, x_ref), (m_hbm, m_ref)))
    ]
    for load in loads:
        load.start()
    blocks, kept = sec_ref.shape[:2]
    per = kept // GROUP
    half = kept // 2
    z = flat(idx_ref)
    tab = tab_ref[...]
    hi, lo = split(tab)
    g = g_ref[...]
    gt_ref[...] = g.T
    row_g = (mm_t(hi, g) + mm_t(lo, g)) * (1.0 / decay_rate)
    ghi, glo = split(row_g)
    rhi, rlo = split(tab[:, :LANES] + tab[:, LANES:])
    row_tab = jnp.concatenate([rhi, ghi, rlo, glo], axis=1)
    chi, clo = split(tab[:SPAN, :LANES] + tab[SPAN : 2 * SPAN, :LANES])
    col_tab = jnp.concatenate([chi, clo], axis=0)
    lane = lax.broadcasted_iota(jnp.int32, (kept, LANES), 1)
    row = lax.broadcasted_iota(jnp.int32, (kept, LANES), 0)
    place = lane - SPAN * ((row // per) & 1)
    lane_in = lane & (SPAN - 1)
    mine = (lane // SPAN) == ((row // (per // GROUP)) & 1)
    none = jnp.zeros((half, LANES), bf16)
    for j in range(blocks):
        col = column(z, j)
        one = jnp.where((col >> 6) == place, 1.0, 0.0).astype(bf16)
        one_a = jnp.concatenate(
            [jnp.concatenate([one[:half], none], axis=1), jnp.concatenate([none, one[half:]], axis=1)], axis=0
        )
        rows = mm(one_a, row_tab).astype(bf16)
        for p in range(2):
            at = slice(p * half, (p + 1) * half)
            sel_ref[j, p, :half, :] = rows[at, :SIDE]
            sel_ref[j, p, half:, :] = rows[at, SIDE:]
            lt_ref[j, p] = jnp.concatenate([rows[at, :LANES], rows[at, SIDE : SIDE + LANES]], axis=0).T
        one_b = jnp.where((col & (SPAN - 1)) == lane_in, 1.0, 0.0).astype(bf16)
        sec_ref[j] = jnp.where(mine, mm(one_b, col_tab), 0.0)
    for load in loads:
        load.wait()


def plan(idx, g, tab, m, x):
    nrow, keep, ncol = idx.shape
    blocks, kept = ncol // GROUP, GROUP * GROUP * keep
    tok = g.shape[0]
    return call(
        plan_kernel,
        "plan",
        flops=2 * 10**9,
        nbytes=4 * 10**6,
        in_specs=whole(3) + anywhere(2),
        out_specs=whole(6),
        out_shape=[
            VMEM((blocks, 2, kept, LANES + tok), bf16),
            VMEM((blocks, kept, LANES), f32),
            VMEM((blocks, 2, LANES, kept), bf16),
            VMEM((g.shape[1], tok), bf16),
            VMEM(m.shape, bf16),
            VMEM(x.shape, bf16),
        ],
        scratch_shapes=[pltpu.SemaphoreType.DMA((2,))],
    )(*vmem(idx, g, tab), *hbm(m, x))


def pick(t_ref, own_ref, peer_ref, j, half):
    h, at = divmod(j, half)
    cols = slice(at * SIDE, (at + 1) * SIDE)
    return jnp.where(t_ref[0] == h, own_ref[:, cols], peer_ref[:, cols])


def select_kernel(t_ref, sel_ref, sec_ref, m_ref, own_ref, peer_ref, out_ref):
    blocks, kept = sec_ref.shape[:2]
    nrow, keep, ncol = out_ref.shape
    half = kept // 2
    lane = lax.broadcasted_iota(jnp.int32, (nrow * keep, LANES), 1)
    acc = jnp.zeros((nrow * keep, LANES), f32)
    for j in range(blocks):
        x = pick(t_ref, own_ref, peer_ref, j, blocks // 2)
        parts = []
        for p in range(2):
            m = m_ref[p * LANES : (p + 1) * LANES, j * SIDE : (j + 1) * SIDE]
            r = mm(sel_ref[j, p], jnp.concatenate([m, x], axis=0))
            for n in range(0, half, ROWS):
                at = slice(0, LANES) if (n // ROWS) % 2 == 0 else slice(LANES, SIDE)
                parts.append(r[n : n + ROWS, at] + r[half + n : half + n + ROWS, at])
        r = jnp.concatenate(parts, axis=0) * sec_ref[j]
        total = jnp.broadcast_to(jnp.sum(r, axis=1, keepdims=True), r.shape)
        for c in range(GROUP):
            parts = [total[(i * GROUP + c) * keep : (i * GROUP + c + 1) * keep] for i in range(nrow)]
            acc = jnp.where(lane == j * GROUP + c, jnp.concatenate(parts, axis=0), acc)
    out_ref[...] = (acc * decay_rate)[:, :ncol].reshape(nrow, keep, ncol)


def select(t, sel, sec, m, own, peer, shape):
    return call(
        select_kernel,
        "select",
        flops=10**9,
        nbytes=6 * 10**6,
        in_specs=[SCALAR] + whole(5),
        out_specs=whole(1)[0],
        out_shape=VMEM(shape, f32),
    )(t, *vmem(sel, sec, m, own, peer))


def decoded(lt, sec, col):
    parts = split(sec * col)
    half = sec.shape[0] // 2
    none = jnp.zeros((ROWS, LANES), bf16)
    outs = []
    for p in range(2):
        wide = []
        for part in parts:
            at = [part[n : n + ROWS] for n in range(p * half, (p + 1) * half, ROWS)]
            left = [a if n % 2 == 0 else none for n, a in enumerate(at)]
            right = [none if n % 2 == 0 else a for n, a in enumerate(at)]
            wide.append(jnp.concatenate([jnp.concatenate(left, axis=0), jnp.concatenate(right, axis=0)], axis=1))
        hi, lo = wide
        rhs = jnp.concatenate([hi, hi, lo, jnp.zeros_like(lo)], axis=0)
        outs.append(mm(jnp.concatenate([lt[p], lt[p]], axis=1), rhs))
    return outs


CHUNKS = 10


def store_block(j, blocks, buf, out_ref, sems, copies):
    per = blocks // CHUNKS
    if (j + 1) % per == 0:
        at = pl.ds((j + 1 - per) * SIDE, per * SIDE)
        copies.append(pltpu.make_async_copy(buf.at[:, at], out_ref.at[:, at], sems.at[j // per]))
        copies[-1].start()


def remain_kernel(t_ref, lt_ref, sec_ref, gt_ref, m_ref, own_ref, peer_ref, c_ref, out_ref, buf, sems):
    blocks = lt_ref.shape[0]
    copies = []
    c = -flat(c_ref)
    for j in range(blocks):
        x = pick(t_ref, own_ref, peer_ref, j, blocks // 2)
        cols = slice(j * SIDE, (j + 1) * SIDE)
        grad = mm(gt_ref[...], x)
        less = decoded(lt_ref[j], sec_ref[j], column(c, j))
        for p in range(2):
            at = slice(p * LANES, (p + 1) * LANES)
            moved = decay_rate * m_ref[at, cols].astype(f32) + grad[at]
            buf[at, cols] = (moved + less[p]).astype(bf16)
        store_block(j, blocks, buf, out_ref, sems, copies)
    for copy in copies:
        copy.wait()


def remain(t, lt, sec, gt, m, own, peer, c):
    return call(
        remain_kernel,
        "remain",
        flops=2 * 10**9,
        nbytes=8 * 10**6,
        in_specs=[SCALAR] + whole(7),
        out_specs=anywhere(1)[0],
        out_shape=jax.ShapeDtypeStruct(m.shape, bf16),
        scratch_shapes=[pltpu.VMEM(m.shape, bf16), pltpu.SemaphoreType.DMA((CHUNKS,))],
    )(t, *vmem(lt, sec, gt, m, own, peer, c))


def update_kernel(scale, lt_ref, sec_ref, sum_ref, out_ref, mean_ref, buf, mean, sems):
    blocks = lt_ref.shape[0]
    mean[...] = sum_ref[...] * scale
    copies = [pltpu.make_async_copy(mean, mean_ref, sems.at[CHUNKS])]
    copies[0].start()
    c = flat(mean)
    for j in range(blocks):
        out = decoded(lt_ref[j], sec_ref[j], column(c, j))
        for p in range(2):
            buf[p * LANES : (p + 1) * LANES, j * SIDE : (j + 1) * SIDE] = out[p].astype(bf16)
        store_block(j, blocks, buf, out_ref, sems, copies)
    for copy in copies:
        copy.wait()


def update(lt, sec, total, replicas, shape):
    return call(
        functools.partial(update_kernel, 1.0 / replicas),
        "update",
        flops=10**9,
        nbytes=6 * 10**6,
        in_specs=whole(3),
        out_specs=anywhere(2),
        out_shape=[jax.ShapeDtypeStruct(shape, bf16), jax.ShapeDtypeStruct(total.shape, f32)],
        scratch_shapes=[
            pltpu.VMEM(shape, bf16),
            pltpu.VMEM(total.shape, f32),
            pltpu.SemaphoreType.DMA((CHUNKS + 1,)),
        ],
    )(*vmem(lt, sec, total))


def halves(t_ref, width, at, size):
    t = t_ref[0]
    mine = pl.ds(pl.multiple_of(t * width + at, LANES), size)
    theirs = pl.ds(pl.multiple_of((1 - t) * width + at, LANES), size)
    return mine, theirs


def keys_kernel(t_ref, own_ref, peer_ref, w_ref, dep_ref, out_ref):
    mine, theirs = halves(t_ref, own_ref.shape[1], 0, own_ref.shape[1])
    out_ref[...] = (mm_t(own_ref[...], w_ref[:, mine]) + mm_t(peer_ref[...], w_ref[:, theirs])).astype(bf16)


def keys_of(t, own, peer, w, dep):
    return call(
        keys_kernel,
        "keys",
        flops=2 * own.shape[0] * w.shape[0] * w.shape[1],
        nbytes=4 * 10**6,
        in_specs=[SCALAR] + whole(3) + anywhere(1),
        out_specs=whole(1)[0],
        out_shape=jax.ShapeDtypeStruct((own.shape[0], w.shape[0]), bf16),
    )(t, *vmem(own, peer, w), dep)


def input_kernel(t_ref, own_ref, peer_ref, w_ref, wp_ref, dep_ref, out_ref, buf, sems):
    width = out_ref.shape[1]
    g = jnp.concatenate([own_ref[...], peer_ref[...]], axis=1)
    copies = []
    per = width // (sems.shape[0] * SIDE)
    for n, at in enumerate(range(0, width, SIDE)):
        mine, _ = halves(t_ref, width, at, SIDE)
        w = jnp.concatenate([w_ref[:, mine], wp_ref[:, mine]], axis=0)
        buf[:, at : at + SIDE] = mm(g, w).astype(bf16)
        if (n + 1) % per == 0:
            cols = pl.ds((n + 1 - per) * SIDE, per * SIDE)
            copies.append(pltpu.make_async_copy(buf.at[:, cols], out_ref.at[:, cols], sems.at[n // per]))
            copies[-1].start()
    for copy in copies:
        copy.wait()


def input_of(t, own, peer, w, wp, dep):
    shape = (own.shape[0], w.shape[1] // 2)
    return call(
        input_kernel,
        "input_grad",
        flops=2 * own.shape[0] * w.shape[0] * w.shape[1],
        nbytes=4 * 10**6,
        in_specs=[SCALAR] + whole(4) + anywhere(1),
        out_specs=anywhere(1)[0],
        out_shape=jax.ShapeDtypeStruct(shape, bf16),
        scratch_shapes=[pltpu.VMEM(shape, bf16), pltpu.SemaphoreType.DMA((5,))],
    )(t, *vmem(own, peer, w, wp), dep)


def shards(tokens, cotangent, key_weight, momentum, indices):
    replicas = lax.axis_size("replica")
    swap = [(0, 1), (1, 0)]
    t = lax.axis_index("tensor").astype(jnp.int32).reshape(1)
    peer = lax.ppermute(tokens, "tensor", swap)
    m = momentum[0]
    idx = indices.transpose(0, 2, 1)
    sel, sec, lt, gt, m_in, own = plan(idx, cotangent, block_table(), m, tokens)
    cot_peer = lax.ppermute(cotangent, "tensor", swap)
    w_peer = lax.ppermute(lax.optimization_barrier((key_weight, peer))[0], "tensor", swap)
    total = select(t, sel, sec, m_in, own, peer, idx.shape)
    mine = total

    def exchange(x, step):
        return lax.ppermute(x, "replica", [(i, i ^ step) for i in range(replicas)])

    steps = [1 << k for k in range(replicas.bit_length() - 1)]
    got = exchange(total, steps[0])
    keys = keys_of(t, own, peer, key_weight, total)
    total, keys = lax.optimization_barrier((total + got, keys))
    got = exchange(total, steps[1])
    input_grad = input_of(t, cotangent, cot_peer, key_weight, w_peer, total)
    total, input_grad = lax.optimization_barrier((total + got, input_grad))
    got = exchange(total, steps[2])
    remaining = remain(t, lt, sec, gt, m_in, own, peer, mine)
    total = total + got
    for step in steps[3:]:
        total = total + exchange(total, step)
    new_update, pooled = update(lt, sec, total, replicas, m.shape)
    return (keys, input_grad, remaining[None], new_update, pooled.transpose(0, 2, 1))


def solution(mesh):
    placed = (
        P(("groups", "replica"), "tensor"),
        P(("groups", "replica"), "tensor"),
        P("tensor", None),
        P(("groups", "replica"), "tensor", None),
        P("tensor", None, None),
    )
    return jax.shard_map(
        shards,
        mesh=mesh,
        in_specs=placed,
        out_specs=(
            P(("groups", "replica"), "tensor"),
            P(("groups", "replica"), "tensor"),
            P(("groups", "replica"), "tensor", None),
            P(("groups", "tensor"), None),
            P(("groups", "tensor"), None, None),
        ),
        check_vma=False,
    )
```

```python
import functools

import jax
import jax.numpy as jnp
import numpy as np
from jax import lax
from jax.experimental import pallas as pl
from jax.experimental.pallas import tpu as pltpu
from jax.sharding import PartitionSpec as P

SPAN = 64
GROUP = 4
SIDE = SPAN * GROUP
LANES = 128
ROWS = 16
decay_rate = 0.9
bf16 = jnp.bfloat16
f32 = jnp.float32
VMEM = pltpu.VMEM


def split(x):
    hi = x.astype(bf16)
    return hi, (x - hi.astype(f32)).astype(bf16)


def dct_table():
    freq = np.arange(SPAN, dtype=np.float64)[:, None]
    place = np.arange(SPAN, dtype=np.float64)[None, :]
    scale = np.where(freq == 0, np.sqrt(1.0 / SPAN), np.sqrt(2.0 / SPAN))
    table = scale * np.cos(np.pi * (2.0 * place + 1.0) * freq / (2.0 * SPAN))
    return np.tile(table, (1, LANES // SPAN)).astype(np.float32)


def mm(a, b):
    return jnp.dot(a, b, preferred_element_type=f32)


def mm_t(a, b):
    return lax.dot_general(a, b, (((1,), (1,)), ((), ())), preferred_element_type=f32)


def call(kernel, name, flops=0, nbytes=0, **kw):
    return pl.pallas_call(
        kernel,
        name=name,
        compiler_params=pltpu.CompilerParams(vmem_limit_bytes=8 * 2**20),
        cost_estimate=pl.CostEstimate(flops=flops, bytes_accessed=nbytes, transcendentals=0),
        **kw,
    )


def vmem(*xs):
    return [pltpu.with_memory_space_constraint(x, VMEM) for x in xs]


def hbm(*xs):
    return [pltpu.with_memory_space_constraint(x, pltpu.HBM) for x in xs]


def whole(n):
    return [pl.BlockSpec(memory_space=VMEM)] * n


def anywhere(n):
    return [pl.BlockSpec(memory_space=pl.ANY)] * n


SCALAR = pl.BlockSpec(memory_space=pltpu.SMEM)


def column(z, j):
    keep = z.shape[0] // GROUP
    parts = [
        jnp.broadcast_to(z[i * keep : (i + 1) * keep, c : c + 1], (keep, LANES))
        for i in range(GROUP)
        for c in range(j * GROUP, (j + 1) * GROUP)
    ]
    return jnp.concatenate(parts, axis=0)


def flat(ref):
    nrow, keep, ncol = ref.shape
    return ref[...].reshape(nrow * keep, ncol)


def plan_kernel(
    idx_hbm, tab_hbm, g_hbm, x_hbm, m_hbm, sel_ref, sec_ref, lt_ref, gt_ref, m_ref, x_ref, idx_ref, tab_ref, g_ref, sems
):
    pairs = ((idx_hbm, idx_ref), (tab_hbm, tab_ref), (g_hbm, g_ref), (x_hbm, x_ref), (m_hbm, m_ref))
    loads = [pltpu.make_async_copy(src, dst, sems.at[n]) for n, (src, dst) in enumerate(pairs)]
    for load in loads:
        load.start()
    for load in loads[:3]:
        load.wait()
    blocks, kept = sec_ref.shape[:2]
    per = kept // GROUP
    half = kept // 2
    z = flat(idx_ref)
    chi, clo = split(tab_ref[...])
    col_tab = jnp.concatenate([chi, clo], axis=0)
    hi = jnp.concatenate([chi, chi], axis=0)
    lo = jnp.concatenate([clo, clo], axis=0)
    square = (LANES, LANES)
    near = lax.broadcasted_iota(jnp.int32, square, 0) // SPAN == lax.broadcasted_iota(jnp.int32, square, 1) // SPAN
    hi = jnp.where(near, hi, jnp.zeros_like(hi))
    lo = jnp.where(near, lo, jnp.zeros_like(lo))
    g = g_ref[...]
    gt_ref[...] = g.T
    row_g = [mm_t(hi, g[:, at : at + LANES]) + mm_t(lo, g[:, at : at + LANES]) for at in range(0, SIDE, LANES)]
    ghi, glo = split(jnp.concatenate(row_g, axis=0) * (1.0 / decay_rate))
    hi, lo = [jnp.concatenate([part, part], axis=0) for part in (hi, lo)]
    row_tab = jnp.concatenate([hi, ghi, lo, glo], axis=1)
    lane = lax.broadcasted_iota(jnp.int32, (kept, LANES), 1)
    row = lax.broadcasted_iota(jnp.int32, (kept, LANES), 0)
    place = lane - SPAN * ((row // per) & 1)
    lane_in = lane & (SPAN - 1)
    mine = (lane // SPAN) == ((row // (per // GROUP)) & 1)
    none = jnp.zeros((half, LANES), bf16)
    for j in range(blocks):
        col = column(z, j)
        one = jnp.where((col >> 6) == place, 1.0, 0.0).astype(bf16)
        one_a = jnp.concatenate(
            [jnp.concatenate([one[:half], none], axis=1), jnp.concatenate([none, one[half:]], axis=1)], axis=0
        )
        rows = mm(one_a, row_tab).astype(bf16)
        for p in range(2):
            at = slice(p * half, (p + 1) * half)
            sel_ref[j, p, :half, :] = rows[at, :SIDE]
            sel_ref[j, p, half:, :] = rows[at, SIDE:]
            lt_ref[j, p] = jnp.concatenate([rows[at, :LANES], rows[at, SIDE : SIDE + LANES]], axis=0).T
        one_b = jnp.where((col & (SPAN - 1)) == lane_in, 1.0, 0.0).astype(bf16)
        sec_ref[j] = jnp.where(mine, mm(one_b, col_tab), 0.0)
    for load in loads[3:]:
        load.wait()


def plan(idx, g, tab, m, x):
    nrow, keep, ncol = idx.shape
    blocks, kept = ncol // GROUP, GROUP * GROUP * keep
    tok = g.shape[0]
    return call(
        plan_kernel,
        "plan",
        flops=2 * 10**9,
        nbytes=4 * 10**6,
        in_specs=anywhere(5),
        out_specs=whole(6),
        out_shape=[
            VMEM((blocks, 2, kept, LANES + tok), bf16),
            VMEM((blocks, kept, LANES), f32),
            VMEM((blocks, 2, LANES, kept), bf16),
            VMEM((g.shape[1], tok), bf16),
            VMEM(m.shape, bf16),
            VMEM(x.shape, bf16),
        ],
        scratch_shapes=[
            pltpu.VMEM(idx.shape, jnp.int32),
            pltpu.VMEM(tab.shape, f32),
            pltpu.VMEM(g.shape, bf16),
            pltpu.SemaphoreType.DMA((5,)),
        ],
    )(*hbm(idx, tab, g, x, m))


def pick(t_ref, own_ref, peer_ref, j, half):
    h, at = divmod(j, half)
    cols = slice(at * SIDE, (at + 1) * SIDE)
    return jnp.where(t_ref[0] == h, own_ref[:, cols], peer_ref[:, cols])


def select_kernel(t_ref, sel_ref, sec_ref, m_ref, own_ref, peer_ref, out_ref):
    blocks, kept = sec_ref.shape[:2]
    nrow, keep, ncol = out_ref.shape
    half = kept // 2
    lane = lax.broadcasted_iota(jnp.int32, (nrow * keep, LANES), 1)
    acc = jnp.zeros((nrow * keep, LANES), f32)
    for j in range(blocks):
        x = pick(t_ref, own_ref, peer_ref, j, blocks // 2)
        parts = []
        for p in range(2):
            m = m_ref[p * LANES : (p + 1) * LANES, j * SIDE : (j + 1) * SIDE]
            r = mm(sel_ref[j, p], jnp.concatenate([m, x], axis=0))
            for n in range(0, half, ROWS):
                at = slice(0, LANES) if (n // ROWS) % 2 == 0 else slice(LANES, SIDE)
                parts.append(r[n : n + ROWS, at] + r[half + n : half + n + ROWS, at])
        r = jnp.concatenate(parts, axis=0) * sec_ref[j]
        total = jnp.broadcast_to(jnp.sum(r, axis=1, keepdims=True), r.shape)
        for c in range(GROUP):
            parts = [total[(i * GROUP + c) * keep : (i * GROUP + c + 1) * keep] for i in range(nrow)]
            acc = jnp.where(lane == j * GROUP + c, jnp.concatenate(parts, axis=0), acc)
    out_ref[...] = (acc * decay_rate)[:, :ncol].reshape(nrow, keep, ncol)


def select(t, sel, sec, m, own, peer, shape):
    return call(
        select_kernel,
        "select",
        flops=10**9,
        nbytes=6 * 10**6,
        in_specs=[SCALAR] + whole(5),
        out_specs=whole(1)[0],
        out_shape=VMEM(shape, f32),
    )(t, *vmem(sel, sec, m, own, peer))


def decoded(lt, sec, col):
    parts = split(sec * col)
    half = sec.shape[0] // 2
    none = jnp.zeros((ROWS, LANES), bf16)
    outs = []
    for p in range(2):
        wide = []
        for part in parts:
            at = [part[n : n + ROWS] for n in range(p * half, (p + 1) * half, ROWS)]
            left = [a if n % 2 == 0 else none for n, a in enumerate(at)]
            right = [none if n % 2 == 0 else a for n, a in enumerate(at)]
            wide.append(jnp.concatenate([jnp.concatenate(left, axis=0), jnp.concatenate(right, axis=0)], axis=1))
        hi, lo = wide
        rhs = jnp.concatenate([hi, hi, lo, jnp.zeros_like(lo)], axis=0)
        outs.append(mm(jnp.concatenate([lt[p], lt[p]], axis=1), rhs))
    return outs


CHUNKS = 10


def store_block(j, blocks, buf, out_ref, sems, copies):
    per = blocks // CHUNKS
    if (j + 1) % per == 0:
        at = pl.ds((j + 1 - per) * SIDE, per * SIDE)
        copies.append(pltpu.make_async_copy(buf.at[:, at], out_ref.at[:, at], sems.at[j // per]))
        copies[-1].start()


def remain_kernel(t_ref, lt_ref, sec_ref, gt_ref, m_ref, own_ref, peer_ref, c_ref, out_ref, buf, sems):
    blocks = lt_ref.shape[0]
    copies = []
    c = -flat(c_ref)
    for j in range(blocks):
        x = pick(t_ref, own_ref, peer_ref, j, blocks // 2)
        cols = slice(j * SIDE, (j + 1) * SIDE)
        grad = mm(gt_ref[...], x)
        less = decoded(lt_ref[j], sec_ref[j], column(c, j))
        for p in range(2):
            at = slice(p * LANES, (p + 1) * LANES)
            moved = decay_rate * m_ref[at, cols].astype(f32) + grad[at]
            buf[at, cols] = (moved + less[p]).astype(bf16)
        store_block(j, blocks, buf, out_ref, sems, copies)
    for copy in copies:
        copy.wait()


def remain(t, lt, sec, gt, m, own, peer, c):
    return call(
        remain_kernel,
        "remain",
        flops=2 * 10**9,
        nbytes=8 * 10**6,
        in_specs=[SCALAR] + whole(7),
        out_specs=anywhere(1)[0],
        out_shape=jax.ShapeDtypeStruct(m.shape, bf16),
        scratch_shapes=[pltpu.VMEM(m.shape, bf16), pltpu.SemaphoreType.DMA((CHUNKS,))],
    )(t, *vmem(lt, sec, gt, m, own, peer, c))


def update_kernel(scale, lt_ref, sec_ref, sum_ref, out_ref, mean_ref, buf, mean, sems):
    blocks = lt_ref.shape[0]
    mean[...] = sum_ref[...] * scale
    copies = [pltpu.make_async_copy(mean, mean_ref, sems.at[CHUNKS])]
    copies[0].start()
    c = flat(mean)
    for j in range(blocks):
        out = decoded(lt_ref[j], sec_ref[j], column(c, j))
        for p in range(2):
            buf[p * LANES : (p + 1) * LANES, j * SIDE : (j + 1) * SIDE] = out[p].astype(bf16)
        store_block(j, blocks, buf, out_ref, sems, copies)
    for copy in copies:
        copy.wait()


def update(lt, sec, total, replicas, shape):
    return call(
        functools.partial(update_kernel, 1.0 / replicas),
        "update",
        flops=10**9,
        nbytes=6 * 10**6,
        in_specs=whole(3),
        out_specs=anywhere(2),
        out_shape=[jax.ShapeDtypeStruct(shape, bf16), jax.ShapeDtypeStruct(total.shape, f32)],
        scratch_shapes=[
            pltpu.VMEM(shape, bf16),
            pltpu.VMEM(total.shape, f32),
            pltpu.SemaphoreType.DMA((CHUNKS + 1,)),
        ],
    )(*vmem(lt, sec, total))


def halves(t_ref, width, at, size):
    t = t_ref[0]
    mine = pl.ds(pl.multiple_of(t * width + at, LANES), size)
    theirs = pl.ds(pl.multiple_of((1 - t) * width + at, LANES), size)
    return mine, theirs


def keys_kernel(t_ref, own_ref, peer_ref, w_ref, dep_ref, out_ref):
    mine, theirs = halves(t_ref, own_ref.shape[1], 0, own_ref.shape[1])
    out_ref[...] = (mm_t(own_ref[...], w_ref[:, mine]) + mm_t(peer_ref[...], w_ref[:, theirs])).astype(bf16)


def keys_of(t, own, peer, w, dep):
    return call(
        keys_kernel,
        "keys",
        flops=2 * own.shape[0] * w.shape[0] * w.shape[1],
        nbytes=4 * 10**6,
        in_specs=[SCALAR] + whole(3) + anywhere(1),
        out_specs=whole(1)[0],
        out_shape=jax.ShapeDtypeStruct((own.shape[0], w.shape[0]), bf16),
    )(t, *vmem(own, peer, w), dep)


def input_kernel(t_ref, own_ref, peer_ref, w_ref, wp_ref, dep_ref, out_ref, buf, sems):
    width = out_ref.shape[1]
    g = jnp.concatenate([own_ref[...], peer_ref[...]], axis=1)
    copies = []
    per = width // (sems.shape[0] * SIDE)
    for n, at in enumerate(range(0, width, SIDE)):
        mine, _ = halves(t_ref, width, at, SIDE)
        w = jnp.concatenate([w_ref[:, mine], wp_ref[:, mine]], axis=0)
        buf[:, at : at + SIDE] = mm(g, w).astype(bf16)
        if (n + 1) % per == 0:
            cols = pl.ds((n + 1 - per) * SIDE, per * SIDE)
            copies.append(pltpu.make_async_copy(buf.at[:, cols], out_ref.at[:, cols], sems.at[n // per]))
            copies[-1].start()
    for copy in copies:
        copy.wait()


def input_of(t, own, peer, w, wp, dep):
    shape = (own.shape[0], w.shape[1] // 2)
    return call(
        input_kernel,
        "input_grad",
        flops=2 * own.shape[0] * w.shape[0] * w.shape[1],
        nbytes=4 * 10**6,
        in_specs=[SCALAR] + whole(4) + anywhere(1),
        out_specs=anywhere(1)[0],
        out_shape=jax.ShapeDtypeStruct(shape, bf16),
        scratch_shapes=[pltpu.VMEM(shape, bf16), pltpu.SemaphoreType.DMA((5,))],
    )(t, *vmem(own, peer, w, wp), dep)


def shards(tokens, cotangent, key_weight, momentum, indices):
    replicas = lax.axis_size("replica")
    swap = [(0, 1), (1, 0)]
    t = lax.axis_index("tensor").astype(jnp.int32).reshape(1)
    peer = lax.ppermute(tokens, "tensor", swap)
    m = momentum[0]
    idx = indices.transpose(0, 2, 1)
    sel, sec, lt, gt, m_in, own = plan(idx, cotangent, jnp.asarray(dct_table()), m, tokens)
    cot_peer = lax.ppermute(cotangent, "tensor", swap)
    total = select(t, sel, sec, m_in, own, peer, idx.shape)
    mine = total

    def exchange(x, step):
        return lax.ppermute(x, "replica", [(i, i ^ step) for i in range(replicas)])

    steps = [1 << k for k in range(replicas.bit_length() - 1)]
    got = exchange(total, steps[0])
    keys = keys_of(t, own, peer, key_weight, total)
    total, keys, w_out = lax.optimization_barrier((total + got, keys, key_weight))
    w_peer = lax.ppermute(w_out, "tensor", swap)
    got = exchange(total, steps[1])
    remaining = remain(t, lt, sec, gt, m_in, own, peer, mine)
    total, remaining, w_peer = lax.optimization_barrier((total + got, remaining, w_peer))
    got = exchange(total, steps[2])
    input_grad = input_of(t, cotangent, cot_peer, key_weight, w_peer, total)
    total, input_grad = lax.optimization_barrier((total + got, input_grad))
    for step in steps[3:]:
        total = total + exchange(total, step)
    new_update, pooled = update(lt, sec, total, replicas, m.shape)
    return (keys, input_grad, remaining[None], new_update, pooled.transpose(0, 2, 1))


def solution(mesh):
    placed = (
        P(("groups", "replica"), "tensor"),
        P(("groups", "replica"), "tensor"),
        P("tensor", None),
        P(("groups", "replica"), "tensor", None),
        P("tensor", None, None),
    )
    return jax.shard_map(
        shards,
        mesh=mesh,
        in_specs=placed,
        out_specs=(
            P(("groups", "replica"), "tensor"),
            P(("groups", "replica"), "tensor"),
            P(("groups", "replica"), "tensor", None),
            P(("groups", "tensor"), None),
            P(("groups", "tensor"), None, None),
        ),
        check_vma=False,
    )
```

```python
import functools

import jax
import jax.numpy as jnp
import numpy as np
from jax import lax
from jax.experimental import pallas as pl
from jax.experimental.pallas import tpu as pltpu
from jax.sharding import PartitionSpec as P

SPAN = 64
GROUP = 4
SIDE = SPAN * GROUP
LANES = 128
ROWS = 16
decay_rate = 0.9
bf16 = jnp.bfloat16
f32 = jnp.float32
VMEM = pltpu.VMEM


def split(x):
    hi = x.astype(bf16)
    return hi, (x - hi.astype(f32)).astype(bf16)


def dct_table():
    freq = np.arange(SPAN, dtype=np.float64)[:, None]
    place = np.arange(SPAN, dtype=np.float64)[None, :]
    scale = np.where(freq == 0, np.sqrt(1.0 / SPAN), np.sqrt(2.0 / SPAN))
    table = scale * np.cos(np.pi * (2.0 * place + 1.0) * freq / (2.0 * SPAN))
    return np.tile(table, (1, LANES // SPAN)).astype(np.float32)


def mm(a, b):
    return jnp.dot(a, b, preferred_element_type=f32)


def mm_t(a, b):
    return lax.dot_general(a, b, (((1,), (1,)), ((), ())), preferred_element_type=f32)


def call(kernel, name, flops=0, nbytes=0, **kw):
    return pl.pallas_call(
        kernel,
        name=name,
        compiler_params=pltpu.CompilerParams(vmem_limit_bytes=16 * 2**20),
        cost_estimate=pl.CostEstimate(flops=flops, bytes_accessed=nbytes, transcendentals=0),
        **kw,
    )


def vmem(*xs):
    return [pltpu.with_memory_space_constraint(x, VMEM) for x in xs]


def hbm(*xs):
    return [pltpu.with_memory_space_constraint(x, pltpu.HBM) for x in xs]


def whole(n):
    return [pl.BlockSpec(memory_space=VMEM)] * n


def anywhere(n):
    return [pl.BlockSpec(memory_space=pl.ANY)] * n


SCALAR = pl.BlockSpec(memory_space=pltpu.SMEM)


def column(z, j):
    keep = z.shape[0] // GROUP
    parts = [
        jnp.broadcast_to(z[i * keep : (i + 1) * keep, c : c + 1], (keep, LANES))
        for i in range(GROUP)
        for c in range(j * GROUP, (j + 1) * GROUP)
    ]
    return jnp.concatenate(parts, axis=0)


def flat(ref):
    nrow, keep, ncol = ref.shape
    return ref[...].reshape(nrow * keep, ncol)


def plan_kernel(
    idx_hbm, tab_hbm, g_hbm, x_hbm, m_hbm, sel_ref, sec_ref, lt_ref, gt_ref, m_ref, x_ref, idx_ref, tab_ref, g_ref, sems
):
    pairs = ((idx_hbm, idx_ref), (tab_hbm, tab_ref), (g_hbm, g_ref), (x_hbm, x_ref), (m_hbm, m_ref))
    loads = [pltpu.make_async_copy(src, dst, sems.at[n]) for n, (src, dst) in enumerate(pairs)]
    for load in loads:
        load.start()
    for load in loads[:3]:
        load.wait()
    blocks, kept = sec_ref.shape[:2]
    per = kept // GROUP
    half = kept // 2
    z = flat(idx_ref)
    chi, clo = split(tab_ref[...])
    col_tab = jnp.concatenate([chi, clo], axis=0)
    none = jnp.zeros((LANES, LANES), bf16)
    col_tab = jnp.concatenate(
        [jnp.concatenate([col_tab, none], axis=1), jnp.concatenate([none, col_tab], axis=1)], axis=0
    )
    lane = lax.broadcasted_iota(jnp.int32, (kept, LANES), 1)
    row = lax.broadcasted_iota(jnp.int32, (kept, LANES), 0)
    place = lane - SPAN * ((row // per) & 1)
    lane_in = lane & (SPAN - 1)
    mine = (lane // SPAN) == ((row // (per // GROUP)) & 1)
    hi = jnp.concatenate([chi, chi], axis=0)
    lo = jnp.concatenate([clo, clo], axis=0)
    near = lax.broadcasted_iota(jnp.int32, hi.shape, 0) // SPAN == lax.broadcasted_iota(jnp.int32, hi.shape, 1) // SPAN
    hi = jnp.where(near, hi, jnp.zeros_like(hi))
    lo = jnp.where(near, lo, jnp.zeros_like(lo))
    g = g_ref[...]
    row_g = [mm_t(hi, g[:, at : at + LANES]) + mm_t(lo, g[:, at : at + LANES]) for at in range(0, SIDE, LANES)]
    ghi, glo = split(jnp.concatenate(row_g, axis=0) * (1.0 / decay_rate))
    hi, lo = [jnp.concatenate([part, part], axis=0) for part in (hi, lo)]
    row_tab = jnp.concatenate([hi, ghi, lo, glo], axis=1)
    none = jnp.zeros((half, LANES), bf16)
    for j in range(0, blocks, 2):
        cols = [column(z, k) for k in (j, j + 1)]
        one_b = [jnp.where((col & (SPAN - 1)) == lane_in, 1.0, 0.0).astype(bf16) for col in cols]
        sec = mm(jnp.concatenate(one_b, axis=1), col_tab)
        for k in range(2):
            sec_ref[j + k] = jnp.where(mine, sec[:, k * LANES : (k + 1) * LANES], 0.0)
            one = jnp.where((cols[k] >> 6) == place, 1.0, 0.0).astype(bf16)
            one_a = jnp.concatenate(
                [jnp.concatenate([one[:half], none], axis=1), jnp.concatenate([none, one[half:]], axis=1)], axis=0
            )
            rows = mm(one_a, row_tab).astype(bf16)
            for p in range(2):
                at = slice(p * half, (p + 1) * half)
                sel_ref[j + k, p, :half, :] = rows[at, :SIDE]
                sel_ref[j + k, p, half:, :] = rows[at, SIDE:]
                lt_ref[j + k, p] = jnp.concatenate([rows[at, :LANES], rows[at, SIDE : SIDE + LANES]], axis=0).T
    gt_ref[...] = g.T
    for load in loads[3:]:
        load.wait()


def plan(idx, g, tab, m, x):
    nrow, keep, ncol = idx.shape
    blocks, kept = ncol // GROUP, GROUP * GROUP * keep
    tok = g.shape[0]
    return call(
        plan_kernel,
        "plan",
        flops=2 * 10**9,
        nbytes=4 * 10**6,
        in_specs=anywhere(5),
        out_specs=whole(6),
        out_shape=[
            VMEM((blocks, 2, kept, LANES + tok), bf16),
            VMEM((blocks, kept, LANES), f32),
            VMEM((blocks, 2, LANES, kept), bf16),
            VMEM((g.shape[1], tok), bf16),
            VMEM(m.shape, bf16),
            VMEM(x.shape, bf16),
        ],
        scratch_shapes=[
            pltpu.VMEM(idx.shape, jnp.int32),
            pltpu.VMEM(tab.shape, f32),
            pltpu.VMEM(g.shape, bf16),
            pltpu.SemaphoreType.DMA((5,)),
        ],
    )(*hbm(idx, tab, g, x, m))


def pick(t_ref, own_ref, peer_ref, j, half):
    h, at = divmod(j, half)
    cols = slice(at * SIDE, (at + 1) * SIDE)
    return jnp.where(t_ref[0] == h, own_ref[:, cols], peer_ref[:, cols])


def select_kernel(t_ref, sel_ref, sec_ref, m_ref, own_ref, peer_ref, out_ref):
    blocks, kept = sec_ref.shape[:2]
    nrow, keep, ncol = out_ref.shape
    half = kept // 2
    lane = lax.broadcasted_iota(jnp.int32, (nrow * keep, LANES), 1)
    acc = jnp.zeros((nrow * keep, LANES), f32)
    for j in range(blocks):
        x = pick(t_ref, own_ref, peer_ref, j, blocks // 2)
        parts = []
        for p in range(2):
            m = m_ref[p * LANES : (p + 1) * LANES, j * SIDE : (j + 1) * SIDE]
            r = mm(sel_ref[j, p], jnp.concatenate([m, x], axis=0))
            for n in range(0, half, ROWS):
                at = slice(0, LANES) if (n // ROWS) % 2 == 0 else slice(LANES, SIDE)
                parts.append(r[n : n + ROWS, at] + r[half + n : half + n + ROWS, at])
        r = jnp.concatenate(parts, axis=0) * sec_ref[j]
        total = jnp.broadcast_to(jnp.sum(r, axis=1, keepdims=True), r.shape)
        for c in range(GROUP):
            parts = [total[(i * GROUP + c) * keep : (i * GROUP + c + 1) * keep] for i in range(nrow)]
            acc = jnp.where(lane == j * GROUP + c, jnp.concatenate(parts, axis=0), acc)
    out_ref[...] = (acc * decay_rate)[:, :ncol].reshape(nrow, keep, ncol)


def select(t, sel, sec, m, own, peer, shape):
    return call(
        select_kernel,
        "select",
        flops=10**9,
        nbytes=6 * 10**6,
        in_specs=[SCALAR] + whole(5),
        out_specs=whole(1)[0],
        out_shape=VMEM(shape, f32),
    )(t, *vmem(sel, sec, m, own, peer))


def decoded(lt, sec, col):
    parts = split(sec * col)
    half = sec.shape[0] // 2
    none = jnp.zeros((ROWS, LANES), bf16)
    outs = []
    for p in range(2):
        wide = []
        for part in parts:
            at = [part[n : n + ROWS] for n in range(p * half, (p + 1) * half, ROWS)]
            left = [a if n % 2 == 0 else none for n, a in enumerate(at)]
            right = [none if n % 2 == 0 else a for n, a in enumerate(at)]
            wide.append(jnp.concatenate([jnp.concatenate(left, axis=0), jnp.concatenate(right, axis=0)], axis=1))
        hi, lo = wide
        rhs = jnp.concatenate([hi, hi, lo, jnp.zeros_like(lo)], axis=0)
        outs.append(mm(jnp.concatenate([lt[p], lt[p]], axis=1), rhs))
    return outs


class Writer:
    def __init__(self, buf, out, sems):
        self.buf, self.out, self.sems, self.copies = buf, out, sems, []

    def put(self, start, stop):
        at = pl.ds(start * SIDE, (stop - start) * SIDE)
        copy = pltpu.make_async_copy(self.buf.at[:, at], self.out.at[:, at], self.sems.at[len(self.copies)])
        copy.start()
        self.copies.append(copy)

    def wait(self):
        for copy in self.copies:
            copy.wait()


STEP = 2
FIRST = 14


def remain_blocks(t_ref, lt_ref, sec_ref, gt_ref, m_ref, own_ref, peer_ref, c_ref, buf, writer, start, stop):
    blocks = lt_ref.shape[0]
    c = -flat(c_ref)
    for j in range(start, stop):
        x = pick(t_ref, own_ref, peer_ref, j, blocks // 2)
        cols = slice(j * SIDE, (j + 1) * SIDE)
        grad = mm(gt_ref[...], x)
        less = decoded(lt_ref[j], sec_ref[j], column(c, j))
        for p in range(2):
            at = slice(p * LANES, (p + 1) * LANES)
            moved = decay_rate * m_ref[at, cols].astype(f32) + grad[at]
            buf[at, cols] = (moved + less[p]).astype(bf16)
        if (j + 1 - start) % STEP == 0 or j + 1 == stop:
            writer.put(j - (j - start) % STEP, j + 1)


def remain_kernel(stop, *refs):
    *ins, out_ref, buf, sems = refs
    writer = Writer(buf, out_ref, sems)
    remain_blocks(*ins, buf, writer, 0, stop)
    writer.wait()


def remain(stop, t, lt, sec, gt, m, own, peer, c):
    return call(
        functools.partial(remain_kernel, stop),
        "remain",
        flops=2 * 10**9,
        nbytes=8 * 10**6,
        in_specs=[SCALAR] + whole(7),
        out_specs=anywhere(1)[0],
        out_shape=jax.ShapeDtypeStruct(m.shape, bf16),
        scratch_shapes=[pltpu.VMEM(m.shape, bf16), pltpu.SemaphoreType.DMA((stop,))],
    )(t, *vmem(lt, sec, gt, m, own, peer, c))


def finish_kernel(start, *refs):
    *ins, g_ref, w_ref, wp_ref, dep_ref, begun_ref, out_ref, in_ref, buf, in_buf, sems, in_sems = refs
    t_ref = ins[0]
    blocks = ins[1].shape[0]
    writer = Writer(buf, out_ref, sems)
    remain_blocks(*ins, buf, writer, start, blocks)
    width = in_buf.shape[1]
    g = jnp.concatenate([g_ref[...], wp_ref[:, width:].T], axis=1)
    in_writer = Writer(in_buf, in_ref, in_sems)
    for n in range(width // SIDE):
        at = slice(n * SIDE, (n + 1) * SIDE)
        mine, _ = halves(t_ref, width, n * SIDE, SIDE)
        w = jnp.concatenate([w_ref[:, mine], wp_ref[:, at]], axis=0)
        in_buf[:, at] = mm(g, w).astype(bf16)
        if n % STEP == STEP - 1:
            in_writer.put(n + 1 - STEP, n + 1)
    writer.wait()
    in_writer.wait()


def finish(start, begun, t, lt, sec, gt, m, own, peer, c, g, w, wp, dep):
    shape = (g.shape[0], w.shape[1] // 2)
    return call(
        functools.partial(finish_kernel, start),
        "finish",
        flops=10**9,
        nbytes=8 * 10**6,
        in_specs=[SCALAR] + whole(10) + anywhere(2),
        out_specs=anywhere(2),
        out_shape=[jax.ShapeDtypeStruct(m.shape, bf16), jax.ShapeDtypeStruct(shape, bf16)],
        scratch_shapes=[
            pltpu.VMEM(m.shape, bf16),
            pltpu.VMEM(shape, bf16),
            pltpu.SemaphoreType.DMA((lt.shape[0],)),
            pltpu.SemaphoreType.DMA((shape[1] // SIDE,)),
        ],
        input_output_aliases={12: 0},
    )(t, *vmem(lt, sec, gt, m, own, peer, c, g, w, wp), dep, begun)


def update_kernel(scale, lt_ref, sec_ref, sum_ref, out_ref, mean_ref, buf, mean, sems):
    blocks = lt_ref.shape[0]
    mean[...] = sum_ref[...] * scale
    writer = Writer(buf, out_ref, sems)
    pooled = pltpu.make_async_copy(mean, mean_ref, sems.at[blocks])
    pooled.start()
    c = flat(mean)
    for j in range(blocks):
        out = decoded(lt_ref[j], sec_ref[j], column(c, j))
        for p in range(2):
            buf[p * LANES : (p + 1) * LANES, j * SIDE : (j + 1) * SIDE] = out[p].astype(bf16)
        if (j + 1) % STEP == 0:
            writer.put(j + 1 - STEP, j + 1)
    writer.wait()
    pooled.wait()


def update(lt, sec, total, replicas, shape):
    return call(
        functools.partial(update_kernel, 1.0 / replicas),
        "update",
        flops=10**9,
        nbytes=6 * 10**6,
        in_specs=whole(3),
        out_specs=anywhere(2),
        out_shape=[jax.ShapeDtypeStruct(shape, bf16), jax.ShapeDtypeStruct(total.shape, f32)],
        scratch_shapes=[
            pltpu.VMEM(shape, bf16),
            pltpu.VMEM(total.shape, f32),
            pltpu.SemaphoreType.DMA((lt.shape[0] + 1,)),
        ],
    )(*vmem(lt, sec, total))


def halves(t_ref, width, at, size):
    t = t_ref[0]
    mine = pl.ds(pl.multiple_of(t * width + at, LANES), size)
    theirs = pl.ds(pl.multiple_of((1 - t) * width + at, LANES), size)
    return mine, theirs


def keys_kernel(t_ref, own_ref, peer_ref, w_ref, gt_ref, dep_ref, out_ref, part_ref, sems):
    width = own_ref.shape[1]
    mine, theirs = halves(t_ref, width, 0, width)
    copies = [
        pltpu.make_async_copy(w_ref.at[:, theirs], part_ref.at[:, :width], sems.at[0]),
        pltpu.make_async_copy(gt_ref, part_ref.at[:, width:], sems.at[1]),
    ]
    for copy in copies:
        copy.start()
    out_ref[...] = (mm_t(own_ref[...], w_ref[:, mine]) + mm_t(peer_ref[...], w_ref[:, theirs])).astype(bf16)
    for copy in copies:
        copy.wait()


def keys_of(t, own, peer, w, gt, dep):
    return call(
        keys_kernel,
        "keys",
        flops=2 * own.shape[0] * w.shape[0] * w.shape[1],
        nbytes=4 * 10**6,
        in_specs=[SCALAR] + whole(4) + anywhere(1),
        out_specs=whole(1) + anywhere(1),
        out_shape=[
            jax.ShapeDtypeStruct((own.shape[0], w.shape[0]), bf16),
            jax.ShapeDtypeStruct((w.shape[0], own.shape[1] + gt.shape[1]), bf16),
        ],
        scratch_shapes=[pltpu.SemaphoreType.DMA((2,))],
    )(t, *vmem(own, peer, w, gt), dep)


def shards(tokens, cotangent, key_weight, momentum, indices):
    replicas = lax.axis_size("replica")
    swap = [(0, 1), (1, 0)]
    t = lax.axis_index("tensor").astype(jnp.int32).reshape(1)
    peer = lax.ppermute(tokens, "tensor", swap)
    m = momentum[0]
    idx = indices.transpose(0, 2, 1)
    tab = jnp.asarray(dct_table())
    sel, sec, lt, gt, m_in, own = plan(idx, cotangent, tab, m, tokens)
    total = select(t, sel, sec, m_in, own, peer, idx.shape)
    mine = total

    def exchange(x, step):
        return lax.ppermute(x, "replica", [(i, i ^ step) for i in range(replicas)])

    steps = [1 << k for k in range(replicas.bit_length() - 1)]
    split_at = FIRST
    got = exchange(total, steps[0])
    keys, w_part = keys_of(t, own, peer, key_weight, gt, total)
    total, keys, w_part = lax.optimization_barrier((total + got, keys, w_part))
    w_peer = lax.ppermute(w_part, "tensor", swap)
    got = exchange(total, steps[1])
    begun = remain(split_at, t, lt, sec, gt, m_in, own, peer, mine)
    total, begun, w_peer = lax.optimization_barrier((total + got, begun, w_peer))
    got = exchange(total, steps[2])
    remaining, input_grad = finish(
        split_at, begun, t, lt, sec, gt, m_in, own, peer, mine, cotangent, key_weight, w_peer, total
    )
    total, input_grad = lax.optimization_barrier((total + got, input_grad))
    for step in steps[3:]:
        total = total + exchange(total, step)
    new_update, pooled = update(lt, sec, total, replicas, m.shape)
    return (keys, input_grad, remaining[None], new_update, pooled.transpose(0, 2, 1))


def solution(mesh):
    placed = (
        P(("groups", "replica"), "tensor"),
        P(("groups", "replica"), "tensor"),
        P("tensor", None),
        P(("groups", "replica"), "tensor", None),
        P("tensor", None, None),
    )
    return jax.shard_map(
        shards,
        mesh=mesh,
        in_specs=placed,
        out_specs=(
            P(("groups", "replica"), "tensor"),
            P(("groups", "replica"), "tensor"),
            P(("groups", "replica"), "tensor", None),
            P(("groups", "tensor"), None),
            P(("groups", "tensor"), None, None),
        ),
        check_vma=False,
    )
```

```python
import functools

import jax
import jax.numpy as jnp
import numpy as np
from jax import lax
from jax.experimental import pallas as pl
from jax.experimental.pallas import tpu as pltpu
from jax.sharding import PartitionSpec as P

SPAN = 64
GROUP = 4
SIDE = SPAN * GROUP
LANES = 128
ROWS = 16
decay_rate = 0.9
bf16 = jnp.bfloat16
f32 = jnp.float32
VMEM = pltpu.VMEM


def split(x):
    hi = x.astype(bf16)
    return hi, (x - hi.astype(f32)).astype(bf16)


def dct_table():
    freq = np.arange(SPAN, dtype=np.float64)[:, None]
    place = np.arange(SPAN, dtype=np.float64)[None, :]
    scale = np.where(freq == 0, np.sqrt(1.0 / SPAN), np.sqrt(2.0 / SPAN))
    table = scale * np.cos(np.pi * (2.0 * place + 1.0) * freq / (2.0 * SPAN))
    return np.tile(table, (1, LANES // SPAN)).astype(np.float32)


def mm(a, b):
    return jnp.dot(a, b, preferred_element_type=f32)


def mm_t(a, b):
    return lax.dot_general(a, b, (((1,), (1,)), ((), ())), preferred_element_type=f32)


def call(kernel, name, flops=0, nbytes=0, **kw):
    return pl.pallas_call(
        kernel,
        name=name,
        compiler_params=pltpu.CompilerParams(vmem_limit_bytes=16 * 2**20),
        cost_estimate=pl.CostEstimate(flops=flops, bytes_accessed=nbytes, transcendentals=0),
        **kw,
    )


def vmem(*xs):
    return [pltpu.with_memory_space_constraint(x, VMEM) for x in xs]


def hbm(*xs):
    return [pltpu.with_memory_space_constraint(x, pltpu.HBM) for x in xs]


def whole(n):
    return [pl.BlockSpec(memory_space=VMEM)] * n


def anywhere(n):
    return [pl.BlockSpec(memory_space=pl.ANY)] * n


SCALAR = pl.BlockSpec(memory_space=pltpu.SMEM)


def column(z, j):
    keep = z.shape[0] // GROUP
    parts = [
        jnp.broadcast_to(z[i * keep : (i + 1) * keep, c : c + 1], (keep, LANES))
        for i in range(GROUP)
        for c in range(j * GROUP, (j + 1) * GROUP)
    ]
    return jnp.concatenate(parts, axis=0)


def flat(ref):
    nrow, keep, ncol = ref.shape
    return ref[...].reshape(nrow * keep, ncol)


def plan_kernel(
    idx_hbm, tab_hbm, g_hbm, x_hbm, m_hbm, sel_ref, sec_ref, lt_ref, gt_ref, m_ref, x_ref, idx_ref, tab_ref, g_ref, sems
):
    pairs = ((idx_hbm, idx_ref), (tab_hbm, tab_ref), (g_hbm, g_ref), (x_hbm, x_ref), (m_hbm, m_ref))
    loads = [pltpu.make_async_copy(src, dst, sems.at[n]) for n, (src, dst) in enumerate(pairs)]
    for load in loads:
        load.start()
    for load in loads[:3]:
        load.wait()
    blocks, kept = sec_ref.shape[:2]
    per = kept // GROUP
    half = kept // 2
    z = flat(idx_ref)
    chi, clo = split(tab_ref[...])
    col_tab = jnp.concatenate([chi, clo], axis=0)
    none = jnp.zeros((LANES, LANES), bf16)
    col_tab = jnp.concatenate(
        [jnp.concatenate([col_tab, none], axis=1), jnp.concatenate([none, col_tab], axis=1)], axis=0
    )
    lane = lax.broadcasted_iota(jnp.int32, (kept, LANES), 1)
    row = lax.broadcasted_iota(jnp.int32, (kept, LANES), 0)
    place = lane - SPAN * ((row // per) & 1)
    lane_in = lane & (SPAN - 1)
    mine = (lane // SPAN) == ((row // (per // GROUP)) & 1)
    hi = jnp.concatenate([chi, chi], axis=0)
    lo = jnp.concatenate([clo, clo], axis=0)
    near = lax.broadcasted_iota(jnp.int32, hi.shape, 0) // SPAN == lax.broadcasted_iota(jnp.int32, hi.shape, 1) // SPAN
    hi = jnp.where(near, hi, jnp.zeros_like(hi))
    lo = jnp.where(near, lo, jnp.zeros_like(lo))
    g = g_ref[...]
    row_g = [mm_t(hi, g[:, at : at + LANES]) + mm_t(lo, g[:, at : at + LANES]) for at in range(0, SIDE, LANES)]
    ghi, glo = split(jnp.concatenate(row_g, axis=0) * (1.0 / decay_rate))
    hi, lo = [jnp.concatenate([part, part], axis=0) for part in (hi, lo)]
    row_tab = jnp.concatenate([hi, ghi, lo, glo], axis=1)
    none = jnp.zeros((half, LANES), bf16)
    for j in range(0, blocks, 2):
        cols = [column(z, k) for k in (j, j + 1)]
        one_b = [jnp.where((col & (SPAN - 1)) == lane_in, 1.0, 0.0).astype(bf16) for col in cols]
        sec = mm(jnp.concatenate(one_b, axis=1), col_tab)
        for k in range(2):
            sec_ref[j + k] = jnp.where(mine, sec[:, k * LANES : (k + 1) * LANES], 0.0)
            one = jnp.where((cols[k] >> 6) == place, 1.0, 0.0).astype(bf16)
            one_a = jnp.concatenate(
                [jnp.concatenate([one[:half], none], axis=1), jnp.concatenate([none, one[half:]], axis=1)], axis=0
            )
            rows = mm(one_a, row_tab).astype(bf16)
            for p in range(2):
                at = slice(p * half, (p + 1) * half)
                sel_ref[j + k, p, :half, :] = rows[at, :SIDE]
                sel_ref[j + k, p, half:, :] = rows[at, SIDE:]
                lt_ref[j + k, p] = jnp.concatenate([rows[at, :LANES], rows[at, SIDE : SIDE + LANES]], axis=0).T
    gt_ref[...] = g.T
    for load in loads[3:]:
        load.wait()


def plan(idx, g, tab, m, x):
    nrow, keep, ncol = idx.shape
    blocks, kept = ncol // GROUP, GROUP * GROUP * keep
    tok = g.shape[0]
    return call(
        plan_kernel,
        "plan",
        flops=2 * 10**9,
        nbytes=4 * 10**6,
        in_specs=anywhere(5),
        out_specs=whole(6),
        out_shape=[
            VMEM((blocks, 2, kept, LANES + tok), bf16),
            VMEM((blocks, kept, LANES), f32),
            VMEM((blocks, 2, LANES, kept), bf16),
            VMEM((g.shape[1], tok), bf16),
            VMEM(m.shape, bf16),
            VMEM(x.shape, bf16),
        ],
        scratch_shapes=[
            pltpu.VMEM(idx.shape, jnp.int32),
            pltpu.VMEM(tab.shape, f32),
            pltpu.VMEM(g.shape, bf16),
            pltpu.SemaphoreType.DMA((5,)),
        ],
    )(*hbm(idx, tab, g, x, m))


def pick(t_ref, own_ref, peer_ref, j, half):
    h, at = divmod(j, half)
    cols = slice(at * SIDE, (at + 1) * SIDE)
    return jnp.where(t_ref[0] == h, own_ref[:, cols], peer_ref[:, cols])


def select_kernel(t_ref, sel_ref, sec_ref, m_ref, own_ref, peer_ref, out_ref):
    blocks, kept = sec_ref.shape[:2]
    nrow, keep, ncol = out_ref.shape
    half = kept // 2
    lane = lax.broadcasted_iota(jnp.int32, (nrow * keep, LANES), 1)
    acc = jnp.zeros((nrow * keep, LANES), f32)
    for j in range(blocks):
        x = pick(t_ref, own_ref, peer_ref, j, blocks // 2)
        parts = []
        for p in range(2):
            m = m_ref[p * LANES : (p + 1) * LANES, j * SIDE : (j + 1) * SIDE]
            r = mm(sel_ref[j, p], jnp.concatenate([m, x], axis=0))
            for n in range(0, half, ROWS):
                at = slice(0, LANES) if (n // ROWS) % 2 == 0 else slice(LANES, SIDE)
                parts.append(r[n : n + ROWS, at] + r[half + n : half + n + ROWS, at])
        r = jnp.concatenate(parts, axis=0) * sec_ref[j]
        total = jnp.broadcast_to(jnp.sum(r, axis=1, keepdims=True), r.shape)
        for c in range(GROUP):
            parts = [total[(i * GROUP + c) * keep : (i * GROUP + c + 1) * keep] for i in range(nrow)]
            acc = jnp.where(lane == j * GROUP + c, jnp.concatenate(parts, axis=0), acc)
    out_ref[...] = (acc * decay_rate)[:, :ncol].reshape(nrow, keep, ncol)


def select(t, sel, sec, m, own, peer, shape):
    return call(
        select_kernel,
        "select",
        flops=10**9,
        nbytes=6 * 10**6,
        in_specs=[SCALAR] + whole(5),
        out_specs=whole(1)[0],
        out_shape=VMEM(shape, f32),
    )(t, *vmem(sel, sec, m, own, peer))


def decoded(lt, sec, col):
    parts = split(sec * col)
    half = sec.shape[0] // 2
    none = jnp.zeros((ROWS, LANES), bf16)
    outs = []
    for p in range(2):
        wide = []
        for part in parts:
            at = [part[n : n + ROWS] for n in range(p * half, (p + 1) * half, ROWS)]
            left = [a if n % 2 == 0 else none for n, a in enumerate(at)]
            right = [none if n % 2 == 0 else a for n, a in enumerate(at)]
            wide.append(jnp.concatenate([jnp.concatenate(left, axis=0), jnp.concatenate(right, axis=0)], axis=1))
        hi, lo = wide
        rhs = jnp.concatenate([hi, hi, lo, jnp.zeros_like(lo)], axis=0)
        outs.append(mm(jnp.concatenate([lt[p], lt[p]], axis=1), rhs))
    return outs


def halves(t_ref, width, at, size):
    t = t_ref[0]
    mine = pl.ds(pl.multiple_of(t * width + at, LANES), size)
    theirs = pl.ds(pl.multiple_of((1 - t) * width + at, LANES), size)
    return mine, theirs


class Writer:
    def __init__(self, sems):
        self.sems, self.copies = sems, []

    def put(self, src, dst):
        copy = pltpu.make_async_copy(src, dst, self.sems.at[len(self.copies)])
        copy.start()
        self.copies.append(copy)

    def wait(self):
        for copy in self.copies:
            copy.wait()


STEP = 2
HEAD = 6
BODY = 12
CARRY = 2


def columns(start, stop):
    return pl.ds(start * SIDE, (stop - start) * SIDE)


def remain_block(refs, j, put):
    t_ref, lt_ref, sec_ref, gt_ref, m_ref, own_ref, peer_ref, c_ref = refs
    x = pick(t_ref, own_ref, peer_ref, j, lt_ref.shape[0] // 2)
    cols = slice(j * SIDE, (j + 1) * SIDE)
    grad = mm(gt_ref[...], x)
    less = decoded(lt_ref[j], sec_ref[j], column(-flat(c_ref), j))
    for p in range(2):
        at = slice(p * LANES, (p + 1) * LANES)
        moved = decay_rate * m_ref[at, cols].astype(f32) + grad[at]
        put(at, (moved + less[p]).astype(bf16))


def store_at(ref, n):
    def put(at, value):
        ref[at, n * SIDE : (n + 1) * SIDE] = value

    return put


def keys_kernel(*refs):
    *ins, w_ref, out_ref, part_ref, head_ref = refs
    t_ref, gt_ref, own_ref, peer_ref = ins[0], ins[3], ins[5], ins[6]
    width = own_ref.shape[1]
    mine, theirs = halves(t_ref, width, 0, width)
    away = w_ref[:, theirs]
    part_ref[:, :width] = away
    part_ref[:, width:] = gt_ref[...]
    out_ref[...] = (mm_t(w_ref[:, mine], own_ref[...]) + mm_t(away, peer_ref[...])).T.astype(bf16)
    for j in range(HEAD):
        remain_block(ins, j, store_at(head_ref, j))


def keys_of(t, lt, sec, gt, m, own, peer, c, w):
    return call(
        keys_kernel,
        "keys",
        flops=10**9,
        nbytes=4 * 10**6,
        in_specs=[SCALAR] + whole(8),
        out_specs=whole(3),
        out_shape=[
            VMEM((own.shape[0], w.shape[0]), bf16),
            VMEM((w.shape[0], own.shape[1] + gt.shape[1]), bf16),
            VMEM((m.shape[0], HEAD * SIDE), bf16),
        ],
    )(t, *vmem(lt, sec, gt, m, own, peer, c, w))


def remain_kernel(*refs):
    *ins, keys_ref, head_ref, keys_out, out_ref, carry_ref, buf, sems = refs
    writer = Writer(sems)
    writer.put(head_ref, out_ref.at[:, columns(0, HEAD)])
    writer.put(keys_ref, keys_out)
    stop = HEAD + BODY - CARRY
    begun = HEAD
    for j in range(HEAD, stop):
        remain_block(ins, j, store_at(buf, j))
        if (j + 1 - begun) == STEP or j + 1 == stop:
            at = columns(begun, j + 1)
            writer.put(buf.at[:, at], out_ref.at[:, at])
            begun = j + 1
    for n in range(CARRY):
        remain_block(ins, stop + n, store_at(carry_ref, n))
    writer.wait()


def remain(t, lt, sec, gt, m, own, peer, c, keys, head):
    return call(
        remain_kernel,
        "remain",
        flops=2 * 10**10,
        nbytes=8 * 10**6,
        in_specs=[SCALAR] + whole(9),
        out_specs=anywhere(2) + whole(1),
        out_shape=[
            jax.ShapeDtypeStruct(keys.shape, bf16),
            jax.ShapeDtypeStruct(m.shape, bf16),
            VMEM((m.shape[0], CARRY * SIDE), bf16),
        ],
        scratch_shapes=[pltpu.VMEM(m.shape, bf16), pltpu.SemaphoreType.DMA((BODY + 2,))],
    )(t, *vmem(lt, sec, gt, m, own, peer, c, keys, head))


def finish_kernel(*refs):
    *ins, carry_ref, g_ref, w_ref, dep_ref, begun_ref, out_ref, part_ref, buf, sems = refs
    t_ref = ins[0]
    blocks = ins[1].shape[0]
    start = HEAD + BODY
    writer = Writer(sems)
    writer.put(carry_ref, out_ref.at[:, columns(start - CARRY, start)])
    begun = start
    for j in range(start, blocks):
        remain_block(ins, j, store_at(buf, j))
        if (j + 1 - begun) == STEP or j + 1 == blocks:
            at = columns(begun, j + 1)
            writer.put(buf.at[:, at], out_ref.at[:, at])
            begun = j + 1
    width = part_ref.shape[1]
    for n in range(width // SIDE):
        mine, _ = halves(t_ref, width, n * SIDE, SIDE)
        part_ref[:, n * SIDE : (n + 1) * SIDE] = mm(g_ref[...], w_ref[:, mine])
    writer.wait()


def finish(begun, t, lt, sec, gt, m, own, peer, c, carry, g, w, dep):
    return call(
        finish_kernel,
        "finish",
        flops=10**9,
        nbytes=8 * 10**6,
        in_specs=[SCALAR] + whole(10) + anywhere(2),
        out_specs=anywhere(1) + whole(1),
        out_shape=[jax.ShapeDtypeStruct(m.shape, bf16), VMEM((g.shape[0], w.shape[1] // 2), f32)],
        scratch_shapes=[pltpu.VMEM(m.shape, bf16), pltpu.SemaphoreType.DMA((lt.shape[0],))],
        input_output_aliases={12: 0},
    )(t, *vmem(lt, sec, gt, m, own, peer, c, carry, g, w), dep, begun)


def update_kernel(scale, lt_ref, sec_ref, sum_ref, part_ref, wp_ref, out_ref, mean_ref, in_ref, buf, mean, in_buf, sems):
    blocks = lt_ref.shape[0]
    mean[...] = sum_ref[...] * scale
    writer = Writer(sems)
    writer.put(mean, mean_ref)
    c = flat(mean)
    width = in_buf.shape[1]
    g = wp_ref[:, width:].T
    for n in range(width // SIDE):
        at = slice(n * SIDE, (n + 1) * SIDE)
        in_buf[:, at] = (part_ref[:, at] + mm(g, wp_ref[:, at])).astype(bf16)
        if n % STEP == STEP - 1:
            at = columns(n + 1 - STEP, n + 1)
            writer.put(in_buf.at[:, at], in_ref.at[:, at])
    begun = 0
    for j in range(blocks):
        out = decoded(lt_ref[j], sec_ref[j], column(c, j))
        for p in range(2):
            buf[p * LANES : (p + 1) * LANES, j * SIDE : (j + 1) * SIDE] = out[p].astype(bf16)
        if j == 0 or (j + 1 - begun) == STEP or j + 1 == blocks:
            at = columns(begun, j + 1)
            writer.put(buf.at[:, at], out_ref.at[:, at])
            begun = j + 1
    writer.wait()


def update(lt, sec, total, part, wp, replicas, shape):
    blocks = lt.shape[0]
    assert blocks * SIDE == 2 * part.shape[1]
    return call(
        functools.partial(update_kernel, 1.0 / replicas),
        "update",
        flops=10**9,
        nbytes=6 * 10**6,
        in_specs=whole(5),
        out_specs=anywhere(3),
        out_shape=[
            jax.ShapeDtypeStruct(shape, bf16),
            jax.ShapeDtypeStruct(total.shape, f32),
            jax.ShapeDtypeStruct(part.shape, bf16),
        ],
        scratch_shapes=[
            pltpu.VMEM(shape, bf16),
            pltpu.VMEM(total.shape, f32),
            pltpu.VMEM(part.shape, bf16),
            pltpu.SemaphoreType.DMA((2 * blocks,)),
        ],
    )(*vmem(lt, sec, total, part, wp))


def shards(tokens, cotangent, key_weight, momentum, indices):
    replicas = lax.axis_size("replica")
    swap = [(0, 1), (1, 0)]
    t = lax.axis_index("tensor").astype(jnp.int32).reshape(1)
    peer = lax.ppermute(tokens, "tensor", swap)
    m = momentum[0]
    idx = indices.transpose(0, 2, 1)
    tab = jnp.asarray(dct_table())
    sel, sec, lt, gt, m_in, own = plan(idx, cotangent, tab, m, tokens)
    total = select(t, sel, sec, m_in, own, peer, idx.shape)
    mine = total

    rounds = replicas.bit_length() - 1

    def exchange(x, n):
        step = 1 << n
        if rounds > 1 and n in (0, rounds - 1):
            pairs = [(2 * r + c, 2 * (r ^ step) + 1 - c) for r in range(replicas) for c in range(2)]
            return lax.ppermute(x, ("replica", "tensor"), pairs), lax.ppermute(x, "tensor", swap)
        return lax.ppermute(x, "replica", [(r, r ^ step) for r in range(replicas)]), x

    shared = (t, lt, sec, gt, m_in, own, peer, mine)
    far, near = exchange(total, 0)
    keys, w_part, head = keys_of(*shared, key_weight)
    total, keys, w_part = lax.optimization_barrier((near + far, keys, w_part))
    for n in range(1, rounds - 2):
        far, near = exchange(total, n)
        total = far + near
    far, near = exchange(total, rounds - 2)
    w_peer = lax.ppermute(w_part, "tensor", swap)
    keys, begun, carry = remain(*shared, keys, head)
    begun, total = lax.optimization_barrier((begun, near + far))
    far, near = exchange(total, rounds - 1)
    remaining, part = finish(begun, *shared, carry, cotangent, key_weight, total)
    remaining, total = lax.optimization_barrier((remaining, near + far))
    new_update, pooled, input_grad = update(lt, sec, total, part, w_peer, replicas, m.shape)
    return (keys, input_grad, remaining[None], new_update, pooled.transpose(0, 2, 1))


def solution(mesh):
    placed = (
        P(("groups", "replica"), "tensor"),
        P(("groups", "replica"), "tensor"),
        P("tensor", None),
        P(("groups", "replica"), "tensor", None),
        P("tensor", None, None),
    )
    return jax.shard_map(
        shards,
        mesh=mesh,
        in_specs=placed,
        out_specs=(
            P(("groups", "replica"), "tensor"),
            P(("groups", "replica"), "tensor"),
            P(("groups", "replica"), "tensor", None),
            P(("groups", "tensor"), None),
            P(("groups", "tensor"), None, None),
        ),
        check_vma=False,
    )
```

```python
import functools

import jax
import jax.numpy as jnp
import numpy as np
from jax import lax
from jax.experimental import pallas as pl
from jax.experimental.pallas import tpu as pltpu
from jax.sharding import PartitionSpec as P

SPAN = 64
GROUP = 4
SIDE = SPAN * GROUP
LANES = 128
ROWS = 16
decay_rate = 0.9
bf16 = jnp.bfloat16
f32 = jnp.float32
VMEM = pltpu.VMEM


def split(x):
    hi = x.astype(bf16)
    return hi, (x - hi.astype(f32)).astype(bf16)


def dct_table():
    freq = np.arange(SPAN, dtype=np.float64)[:, None]
    place = np.arange(SPAN, dtype=np.float64)[None, :]
    scale = np.where(freq == 0, np.sqrt(1.0 / SPAN), np.sqrt(2.0 / SPAN))
    table = scale * np.cos(np.pi * (2.0 * place + 1.0) * freq / (2.0 * SPAN))
    return np.tile(table, (1, LANES // SPAN)).astype(np.float32)


def mm(a, b):
    return jnp.dot(a, b, preferred_element_type=f32)


def mm_t(a, b):
    return lax.dot_general(a, b, (((1,), (1,)), ((), ())), preferred_element_type=f32)


def call(kernel, name, flops=0, nbytes=0, **kw):
    return pl.pallas_call(
        kernel,
        name=name,
        compiler_params=pltpu.CompilerParams(vmem_limit_bytes=16 * 2**20),
        cost_estimate=pl.CostEstimate(flops=flops, bytes_accessed=nbytes, transcendentals=0),
        **kw,
    )


def vmem(*xs):
    return [pltpu.with_memory_space_constraint(x, VMEM) for x in xs]


def hbm(*xs):
    return [pltpu.with_memory_space_constraint(x, pltpu.HBM) for x in xs]


def whole(n):
    return [pl.BlockSpec(memory_space=VMEM)] * n


def anywhere(n):
    return [pl.BlockSpec(memory_space=pl.ANY)] * n


SCALAR = pl.BlockSpec(memory_space=pltpu.SMEM)


def column(z, j):
    keep = z.shape[0] // GROUP
    parts = [
        jnp.broadcast_to(z[i * keep : (i + 1) * keep, c : c + 1], (keep, LANES))
        for i in range(GROUP)
        for c in range(j * GROUP, (j + 1) * GROUP)
    ]
    return jnp.concatenate(parts, axis=0)


def flat(ref):
    nrow, keep, ncol = ref.shape
    return ref[...].reshape(nrow * keep, ncol)


def plan_kernel(
    idx_hbm, tab_hbm, g_hbm, x_hbm, m_hbm, sel_ref, sec_ref, lt_ref, gt_ref, m_ref, x_ref, idx_ref, tab_ref, g_ref, sems
):
    pairs = ((idx_hbm, idx_ref), (tab_hbm, tab_ref), (g_hbm, g_ref), (x_hbm, x_ref), (m_hbm, m_ref))
    loads = [pltpu.make_async_copy(src, dst, sems.at[n]) for n, (src, dst) in enumerate(pairs)]
    for load in loads:
        load.start()
    for load in loads[:3]:
        load.wait()
    blocks, kept = sec_ref.shape[:2]
    per = kept // GROUP
    half = kept // 2
    z = flat(idx_ref)
    chi, clo = split(tab_ref[...])
    col_tab = jnp.concatenate([chi, clo], axis=0)
    none = jnp.zeros((LANES, LANES), bf16)
    col_tab = jnp.concatenate(
        [jnp.concatenate([col_tab, none], axis=1), jnp.concatenate([none, col_tab], axis=1)], axis=0
    )
    lane = lax.broadcasted_iota(jnp.int32, (kept, LANES), 1)
    row = lax.broadcasted_iota(jnp.int32, (kept, LANES), 0)
    place = lane - SPAN * ((row // per) & 1)
    lane_in = lane & (SPAN - 1)
    mine = (lane // SPAN) == ((row // (per // GROUP)) & 1)
    hi = jnp.concatenate([chi, chi], axis=0)
    lo = jnp.concatenate([clo, clo], axis=0)
    near = lax.broadcasted_iota(jnp.int32, hi.shape, 0) // SPAN == lax.broadcasted_iota(jnp.int32, hi.shape, 1) // SPAN
    hi = jnp.where(near, hi, jnp.zeros_like(hi))
    lo = jnp.where(near, lo, jnp.zeros_like(lo))
    g = g_ref[...]
    row_g = [mm_t(hi, g[:, at : at + LANES]) + mm_t(lo, g[:, at : at + LANES]) for at in range(0, SIDE, LANES)]
    ghi, glo = split(jnp.concatenate(row_g, axis=0) * (1.0 / decay_rate))
    hi, lo = [jnp.concatenate([part, part], axis=0) for part in (hi, lo)]
    row_tab = jnp.concatenate([hi, ghi, lo, glo], axis=1)
    none = jnp.zeros((half, LANES), bf16)
    group = 10
    for j in range(0, blocks, group):
        cols = [column(z, k) for k in range(j, j + group)]
        one_b = [jnp.where((col & (SPAN - 1)) == lane_in, 1.0, 0.0).astype(bf16) for col in cols]
        one_a = []
        for col in cols:
            one = jnp.where((col >> 6) == place, 1.0, 0.0).astype(bf16)
            one_a.append(jnp.concatenate([one[:half], none], axis=1))
            one_a.append(jnp.concatenate([none, one[half:]], axis=1))
        pairs = [jnp.concatenate(one_b[k : k + 2], axis=1) for k in range(0, group, 2)]
        sec = mm(jnp.concatenate(pairs, axis=0), col_tab)
        rows = mm(jnp.concatenate(one_a, axis=0), row_tab).astype(bf16)
        for k in range(group):
            sec_ref[j + k] = jnp.where(mine, sec[k // 2 * kept : (k // 2 + 1) * kept, k % 2 * LANES : (k % 2 + 1) * LANES], 0.0)
            for p in range(2):
                at = slice(k * kept + p * half, k * kept + (p + 1) * half)
                sel_ref[j + k, p, :half, :] = rows[at, :SIDE]
                sel_ref[j + k, p, half:, :] = rows[at, SIDE:]
                lt_ref[j + k, p] = jnp.concatenate([rows[at, :LANES], rows[at, SIDE : SIDE + LANES]], axis=0).T
    gt_ref[...] = g.T
    for load in loads[3:]:
        load.wait()


def plan(idx, g, tab, m, x):
    nrow, keep, ncol = idx.shape
    blocks, kept = ncol // GROUP, GROUP * GROUP * keep
    tok = g.shape[0]
    return call(
        plan_kernel,
        "plan",
        flops=2 * 10**9,
        nbytes=4 * 10**6,
        in_specs=anywhere(5),
        out_specs=whole(6),
        out_shape=[
            VMEM((blocks, 2, kept, LANES + tok), bf16),
            VMEM((blocks, kept, LANES), f32),
            VMEM((blocks, 2, LANES, kept), bf16),
            VMEM((g.shape[1], tok), bf16),
            VMEM(m.shape, bf16),
            VMEM(x.shape, bf16),
        ],
        scratch_shapes=[
            pltpu.VMEM(idx.shape, jnp.int32),
            pltpu.VMEM(tab.shape, f32),
            pltpu.VMEM(g.shape, bf16),
            pltpu.SemaphoreType.DMA((5,)),
        ],
    )(*hbm(idx, tab, g, x, m))


def pick(t_ref, own_ref, peer_ref, j, half):
    h, at = divmod(j, half)
    cols = slice(at * SIDE, (at + 1) * SIDE)
    return jnp.where(t_ref[0] == h, own_ref[:, cols], peer_ref[:, cols])


def select_kernel(t_ref, sel_ref, sec_ref, m_ref, own_ref, peer_ref, out_ref):
    blocks, kept = sec_ref.shape[:2]
    nrow, keep, ncol = out_ref.shape
    half = kept // 2
    lane = lax.broadcasted_iota(jnp.int32, (nrow * keep, LANES), 1)
    acc = jnp.zeros((nrow * keep, LANES), f32)
    for j in range(blocks):
        x = pick(t_ref, own_ref, peer_ref, j, blocks // 2)
        parts = []
        for p in range(2):
            m = m_ref[p * LANES : (p + 1) * LANES, j * SIDE : (j + 1) * SIDE]
            r = mm(sel_ref[j, p], jnp.concatenate([m, x], axis=0))
            for n in range(0, half, ROWS):
                at = slice(0, LANES) if (n // ROWS) % 2 == 0 else slice(LANES, SIDE)
                parts.append(r[n : n + ROWS, at] + r[half + n : half + n + ROWS, at])
        r = jnp.concatenate(parts, axis=0) * sec_ref[j]
        total = jnp.broadcast_to(jnp.sum(r, axis=1, keepdims=True), r.shape)
        for c in range(GROUP):
            parts = [total[(i * GROUP + c) * keep : (i * GROUP + c + 1) * keep] for i in range(nrow)]
            acc = jnp.where(lane == j * GROUP + c, jnp.concatenate(parts, axis=0), acc)
    out_ref[...] = (acc * decay_rate)[:, :ncol].reshape(nrow, keep, ncol)


def select(t, sel, sec, m, own, peer, shape):
    return call(
        select_kernel,
        "select",
        flops=10**9,
        nbytes=6 * 10**6,
        in_specs=[SCALAR] + whole(5),
        out_specs=whole(1)[0],
        out_shape=VMEM(shape, f32),
    )(t, *vmem(sel, sec, m, own, peer))


def decoded(lt, sec, col):
    parts = split(sec * col)
    half = sec.shape[0] // 2
    none = jnp.zeros((ROWS, LANES), bf16)
    outs = []
    for p in range(2):
        wide = []
        for part in parts:
            at = [part[n : n + ROWS] for n in range(p * half, (p + 1) * half, ROWS)]
            left = [a if n % 2 == 0 else none for n, a in enumerate(at)]
            right = [none if n % 2 == 0 else a for n, a in enumerate(at)]
            wide.append(jnp.concatenate([jnp.concatenate(left, axis=0), jnp.concatenate(right, axis=0)], axis=1))
        hi, lo = wide
        rhs = jnp.concatenate([hi, hi, lo, jnp.zeros_like(lo)], axis=0)
        outs.append(mm(jnp.concatenate([lt[p], lt[p]], axis=1), rhs))
    return outs


def halves(t_ref, width, at, size):
    t = t_ref[0]
    mine = pl.ds(pl.multiple_of(t * width + at, LANES), size)
    theirs = pl.ds(pl.multiple_of((1 - t) * width + at, LANES), size)
    return mine, theirs


class Writer:
    def __init__(self, sems):
        self.sems, self.copies = sems, []

    def put(self, src, dst):
        copy = pltpu.make_async_copy(src, dst, self.sems.at[len(self.copies)])
        copy.start()
        self.copies.append(copy)

    def wait(self):
        for copy in self.copies:
            copy.wait()


STEP = 2
HEAD = 6
BODY = 12
CARRY = 2


def columns(start, stop):
    return pl.ds(start * SIDE, (stop - start) * SIDE)


def remain_block(refs, j, put):
    t_ref, lt_ref, sec_ref, gt_ref, m_ref, own_ref, peer_ref, c_ref = refs
    x = pick(t_ref, own_ref, peer_ref, j, lt_ref.shape[0] // 2)
    cols = slice(j * SIDE, (j + 1) * SIDE)
    grad = mm(gt_ref[...], x)
    less = decoded(lt_ref[j], sec_ref[j], column(-flat(c_ref), j))
    for p in range(2):
        at = slice(p * LANES, (p + 1) * LANES)
        moved = decay_rate * m_ref[at, cols].astype(f32) + grad[at]
        put(at, (moved + less[p]).astype(bf16))


def store_at(ref, n):
    def put(at, value):
        ref[at, n * SIDE : (n + 1) * SIDE] = value

    return put


def keys_kernel(*refs):
    *ins, w_ref, out_ref, part_ref, head_ref = refs
    t_ref, gt_ref, own_ref, peer_ref = ins[0], ins[3], ins[5], ins[6]
    width = own_ref.shape[1]
    mine, theirs = halves(t_ref, width, 0, width)
    away = w_ref[:, theirs]
    part_ref[:, :width] = away
    part_ref[:, width:] = gt_ref[...]
    out_ref[...] = (mm_t(w_ref[:, mine], own_ref[...]) + mm_t(away, peer_ref[...])).T.astype(bf16)
    for j in range(HEAD):
        remain_block(ins, j, store_at(head_ref, j))


def keys_of(t, lt, sec, gt, m, own, peer, c, w):
    return call(
        keys_kernel,
        "keys",
        flops=10**9,
        nbytes=4 * 10**6,
        in_specs=[SCALAR] + whole(8),
        out_specs=whole(3),
        out_shape=[
            VMEM((own.shape[0], w.shape[0]), bf16),
            VMEM((w.shape[0], own.shape[1] + gt.shape[1]), bf16),
            VMEM((m.shape[0], HEAD * SIDE), bf16),
        ],
    )(t, *vmem(lt, sec, gt, m, own, peer, c, w))


def remain_kernel(*refs):
    *ins, keys_ref, head_ref, keys_out, out_ref, carry_ref, buf, sems = refs
    writer = Writer(sems)
    writer.put(head_ref, out_ref.at[:, columns(0, HEAD)])
    writer.put(keys_ref, keys_out)
    stop = HEAD + BODY - CARRY
    begun = HEAD
    for j in range(HEAD, stop):
        remain_block(ins, j, store_at(buf, j))
        if (j + 1 - begun) == STEP or j + 1 == stop:
            at = columns(begun, j + 1)
            writer.put(buf.at[:, at], out_ref.at[:, at])
            begun = j + 1
    for n in range(CARRY):
        remain_block(ins, stop + n, store_at(carry_ref, n))
    writer.wait()


def remain(t, lt, sec, gt, m, own, peer, c, keys, head):
    return call(
        remain_kernel,
        "remain",
        flops=2 * 10**10,
        nbytes=8 * 10**6,
        in_specs=[SCALAR] + whole(9),
        out_specs=anywhere(2) + whole(1),
        out_shape=[
            jax.ShapeDtypeStruct(keys.shape, bf16),
            jax.ShapeDtypeStruct(m.shape, bf16),
            VMEM((m.shape[0], CARRY * SIDE), bf16),
        ],
        scratch_shapes=[pltpu.VMEM(m.shape, bf16), pltpu.SemaphoreType.DMA((BODY + 2,))],
    )(t, *vmem(lt, sec, gt, m, own, peer, c, keys, head))


def finish_kernel(*refs):
    *ins, carry_ref, g_ref, w_ref, dep_ref, begun_ref, out_ref, part_ref, buf, sems = refs
    t_ref = ins[0]
    blocks = ins[1].shape[0]
    start = HEAD + BODY
    writer = Writer(sems)
    writer.put(carry_ref, out_ref.at[:, columns(start - CARRY, start)])
    begun = start
    for j in range(start, blocks):
        remain_block(ins, j, store_at(buf, j))
        if (j + 1 - begun) == STEP or j + 1 == blocks:
            at = columns(begun, j + 1)
            writer.put(buf.at[:, at], out_ref.at[:, at])
            begun = j + 1
    width = part_ref.shape[1]
    for n in range(width // SIDE):
        mine, _ = halves(t_ref, width, n * SIDE, SIDE)
        part_ref[:, n * SIDE : (n + 1) * SIDE] = mm(g_ref[...], w_ref[:, mine])
    writer.wait()


def finish(begun, t, lt, sec, gt, m, own, peer, c, carry, g, w, dep):
    return call(
        finish_kernel,
        "finish",
        flops=10**9,
        nbytes=8 * 10**6,
        in_specs=[SCALAR] + whole(10) + anywhere(2),
        out_specs=anywhere(1) + whole(1),
        out_shape=[jax.ShapeDtypeStruct(m.shape, bf16), VMEM((g.shape[0], w.shape[1] // 2), f32)],
        scratch_shapes=[pltpu.VMEM(m.shape, bf16), pltpu.SemaphoreType.DMA((lt.shape[0],))],
        input_output_aliases={12: 0},
    )(t, *vmem(lt, sec, gt, m, own, peer, c, carry, g, w), dep, begun)


def update_kernel(scale, lt_ref, sec_ref, sum_ref, part_ref, wp_ref, out_ref, mean_ref, in_ref, buf, mean, in_buf, sems):
    blocks = lt_ref.shape[0]
    mean[...] = sum_ref[...] * scale
    writer = Writer(sems)
    writer.put(mean, mean_ref)
    c = flat(mean)
    width = in_buf.shape[1]
    g = wp_ref[:, width:].T
    for n in range(width // SIDE):
        at = slice(n * SIDE, (n + 1) * SIDE)
        in_buf[:, at] = (part_ref[:, at] + mm(g, wp_ref[:, at])).astype(bf16)
        if n % STEP == STEP - 1:
            at = columns(n + 1 - STEP, n + 1)
            writer.put(in_buf.at[:, at], in_ref.at[:, at])
    begun = 0
    for j in range(blocks):
        out = decoded(lt_ref[j], sec_ref[j], column(c, j))
        for p in range(2):
            buf[p * LANES : (p + 1) * LANES, j * SIDE : (j + 1) * SIDE] = out[p].astype(bf16)
        if j == 0 or (j + 1 - begun) == STEP or j + 2 >= blocks:
            at = columns(begun, j + 1)
            writer.put(buf.at[:, at], out_ref.at[:, at])
            begun = j + 1
    writer.wait()


def update(lt, sec, total, part, wp, replicas, shape):
    blocks = lt.shape[0]
    assert blocks * SIDE == 2 * part.shape[1]
    return call(
        functools.partial(update_kernel, 1.0 / replicas),
        "update",
        flops=10**9,
        nbytes=6 * 10**6,
        in_specs=whole(5),
        out_specs=anywhere(3),
        out_shape=[
            jax.ShapeDtypeStruct(shape, bf16),
            jax.ShapeDtypeStruct(total.shape, f32),
            jax.ShapeDtypeStruct(part.shape, bf16),
        ],
        scratch_shapes=[
            pltpu.VMEM(shape, bf16),
            pltpu.VMEM(total.shape, f32),
            pltpu.VMEM(part.shape, bf16),
            pltpu.SemaphoreType.DMA((2 * blocks,)),
        ],
    )(*vmem(lt, sec, total, part, wp))


def shards(tokens, cotangent, key_weight, momentum, indices):
    replicas = lax.axis_size("replica")
    swap = [(0, 1), (1, 0)]
    t = lax.axis_index("tensor").astype(jnp.int32).reshape(1)
    peer = lax.ppermute(tokens, "tensor", swap)
    m = momentum[0]
    idx = indices.transpose(0, 2, 1)
    tab = jnp.asarray(dct_table())
    sel, sec, lt, gt, m_in, own = plan(idx, cotangent, tab, m, tokens)
    total = select(t, sel, sec, m_in, own, peer, idx.shape)
    mine = total

    rounds = replicas.bit_length() - 1

    def exchange(x, n):
        step = 1 << n
        if rounds > 1 and n in (0, rounds - 1):
            pairs = [(2 * r + c, 2 * (r ^ step) + 1 - c) for r in range(replicas) for c in range(2)]
            return lax.ppermute(x, ("replica", "tensor"), pairs), lax.ppermute(x, "tensor", swap)
        return lax.ppermute(x, "replica", [(r, r ^ step) for r in range(replicas)]), x

    shared = (t, lt, sec, gt, m_in, own, peer, mine)
    far, near = exchange(total, 0)
    keys, w_part, head = keys_of(*shared, key_weight)
    total, keys, w_part = lax.optimization_barrier((near + far, keys, w_part))
    for n in range(1, rounds - 2):
        far, near = exchange(total, n)
        total = far + near
    far, near = exchange(total, rounds - 2)
    w_peer = lax.ppermute(w_part, "tensor", swap)
    keys, begun, carry = remain(*shared, keys, head)
    begun, total = lax.optimization_barrier((begun, near + far))
    far, near = exchange(total, rounds - 1)
    remaining, part = finish(begun, *shared, carry, cotangent, key_weight, total)
    remaining, total = lax.optimization_barrier((remaining, near + far))
    new_update, pooled, input_grad = update(lt, sec, total, part, w_peer, replicas, m.shape)
    return (keys, input_grad, remaining[None], new_update, pooled.transpose(0, 2, 1))


def solution(mesh):
    placed = (
        P(("groups", "replica"), "tensor"),
        P(("groups", "replica"), "tensor"),
        P("tensor", None),
        P(("groups", "replica"), "tensor", None),
        P("tensor", None, None),
    )
    return jax.shard_map(
        shards,
        mesh=mesh,
        in_specs=placed,
        out_specs=(
            P(("groups", "replica"), "tensor"),
            P(("groups", "replica"), "tensor"),
            P(("groups", "replica"), "tensor", None),
            P(("groups", "tensor"), None),
            P(("groups", "tensor"), None, None),
        ),
        check_vma=False,
    )
```

```python
import functools

import jax
import jax.numpy as jnp
import numpy as np
from jax import lax
from jax.experimental import pallas as pl
from jax.experimental.pallas import tpu as pltpu
from jax.sharding import PartitionSpec as P

SPAN = 64
GROUP = 4
SIDE = SPAN * GROUP
LANES = 128
ROWS = 16
decay_rate = 0.9
bf16 = jnp.bfloat16
f32 = jnp.float32
VMEM = pltpu.VMEM


def split(x):
    hi = x.astype(bf16)
    return hi, (x - hi.astype(f32)).astype(bf16)


def dct_table():
    freq = np.arange(SPAN, dtype=np.float64)[:, None]
    place = np.arange(SPAN, dtype=np.float64)[None, :]
    scale = np.where(freq == 0, np.sqrt(1.0 / SPAN), np.sqrt(2.0 / SPAN))
    table = scale * np.cos(np.pi * (2.0 * place + 1.0) * freq / (2.0 * SPAN))
    return np.tile(table, (1, LANES // SPAN)).astype(np.float32)


def mm(a, b):
    return jnp.dot(a, b, preferred_element_type=f32)


def mm_t(a, b):
    return lax.dot_general(a, b, (((1,), (1,)), ((), ())), preferred_element_type=f32)


def call(kernel, name, flops=0, nbytes=0, **kw):
    return pl.pallas_call(
        kernel,
        name=name,
        compiler_params=pltpu.CompilerParams(vmem_limit_bytes=16 * 2**20),
        cost_estimate=pl.CostEstimate(flops=flops, bytes_accessed=nbytes, transcendentals=0),
        **kw,
    )


def vmem(*xs):
    return [pltpu.with_memory_space_constraint(x, VMEM) for x in xs]


def hbm(*xs):
    return [pltpu.with_memory_space_constraint(x, pltpu.HBM) for x in xs]


def whole(n):
    return [pl.BlockSpec(memory_space=VMEM)] * n


def anywhere(n):
    return [pl.BlockSpec(memory_space=pl.ANY)] * n


SCALAR = pl.BlockSpec(memory_space=pltpu.SMEM)


def column(z, j):
    keep = z.shape[0] // GROUP
    parts = [
        jnp.broadcast_to(z[i * keep : (i + 1) * keep, c : c + 1], (keep, LANES))
        for i in range(GROUP)
        for c in range(j * GROUP, (j + 1) * GROUP)
    ]
    return jnp.concatenate(parts, axis=0)


def flat(ref):
    nrow, keep, ncol = ref.shape
    return ref[...].reshape(nrow * keep, ncol)


def plan_kernel(
    idx_hbm, tab_hbm, g_hbm, x_hbm, m_hbm, sel_ref, sec_ref, lt_ref, gt_ref, m_ref, x_ref, idx_ref, tab_ref, g_ref, sems
):
    pairs = ((idx_hbm, idx_ref), (tab_hbm, tab_ref), (g_hbm, g_ref), (x_hbm, x_ref), (m_hbm, m_ref))
    loads = [pltpu.make_async_copy(src, dst, sems.at[n]) for n, (src, dst) in enumerate(pairs)]
    for load in loads:
        load.start()
    for load in loads[:3]:
        load.wait()
    blocks, kept = sec_ref.shape[:2]
    per = kept // GROUP
    half = kept // 2
    z = flat(idx_ref)
    chi, clo = split(tab_ref[...])
    col_tab = jnp.concatenate([chi, clo], axis=0)
    none = jnp.zeros((LANES, LANES), bf16)
    col_tab = jnp.concatenate(
        [jnp.concatenate([col_tab, none], axis=1), jnp.concatenate([none, col_tab], axis=1)], axis=0
    )
    lane = lax.broadcasted_iota(jnp.int32, (kept, LANES), 1)
    row = lax.broadcasted_iota(jnp.int32, (kept, LANES), 0)
    place = lane - SPAN * ((row // per) & 1)
    lane_in = lane & (SPAN - 1)
    mine = (lane // SPAN) == ((row // (per // GROUP)) & 1)
    hi = jnp.concatenate([chi, chi], axis=0)
    lo = jnp.concatenate([clo, clo], axis=0)
    near = lax.broadcasted_iota(jnp.int32, hi.shape, 0) // SPAN == lax.broadcasted_iota(jnp.int32, hi.shape, 1) // SPAN
    hi = jnp.where(near, hi, jnp.zeros_like(hi))
    lo = jnp.where(near, lo, jnp.zeros_like(lo))
    g = g_ref[...]
    row_g = [mm_t(hi, g[:, at : at + LANES]) + mm_t(lo, g[:, at : at + LANES]) for at in range(0, SIDE, LANES)]
    ghi, glo = split(jnp.concatenate(row_g, axis=0) * (1.0 / decay_rate))
    hi, lo = [jnp.concatenate([part, part], axis=0) for part in (hi, lo)]
    row_tab = jnp.concatenate([hi, ghi, lo, glo], axis=1)
    none = jnp.zeros((half, LANES), bf16)
    group = 10
    for j in range(0, blocks, group):
        cols = [column(z, k) for k in range(j, j + group)]
        one_b = [jnp.where((col & (SPAN - 1)) == lane_in, 1.0, 0.0).astype(bf16) for col in cols]
        one_a = []
        for col in cols:
            one = jnp.where((col >> 6) == place, 1.0, 0.0).astype(bf16)
            one_a.append(jnp.concatenate([one[:half], none], axis=1))
            one_a.append(jnp.concatenate([none, one[half:]], axis=1))
        pairs = [jnp.concatenate(one_b[k : k + 2], axis=1) for k in range(0, group, 2)]
        sec = mm(jnp.concatenate(pairs, axis=0), col_tab)
        rows = mm(jnp.concatenate(one_a, axis=0), row_tab).astype(bf16)
        for k in range(group):
            sec_ref[j + k] = jnp.where(mine, sec[k // 2 * kept : (k // 2 + 1) * kept, k % 2 * LANES : (k % 2 + 1) * LANES], 0.0)
            for p in range(2):
                at = slice(k * kept + p * half, k * kept + (p + 1) * half)
                sel_ref[j + k, p, :half, :] = rows[at, :SIDE]
                sel_ref[j + k, p, half:, :] = rows[at, SIDE:]
                lt_ref[j + k, p] = jnp.concatenate([rows[at, :LANES], rows[at, SIDE : SIDE + LANES]], axis=0).T
    gt_ref[...] = g.T
    for load in loads[3:]:
        load.wait()


def plan(idx, g, tab, m, x):
    nrow, keep, ncol = idx.shape
    blocks, kept = ncol // GROUP, GROUP * GROUP * keep
    tok = g.shape[0]
    return call(
        plan_kernel,
        "plan",
        flops=2 * 10**9,
        nbytes=4 * 10**6,
        in_specs=anywhere(5),
        out_specs=whole(6),
        out_shape=[
            VMEM((blocks, 2, kept, LANES + tok), bf16),
            VMEM((blocks, kept, LANES), f32),
            VMEM((blocks, 2, LANES, kept), bf16),
            VMEM((g.shape[1], tok), bf16),
            VMEM(m.shape, bf16),
            VMEM(x.shape, bf16),
        ],
        scratch_shapes=[
            pltpu.VMEM(idx.shape, jnp.int32),
            pltpu.VMEM(tab.shape, f32),
            pltpu.VMEM(g.shape, bf16),
            pltpu.SemaphoreType.DMA((5,)),
        ],
    )(*hbm(idx, tab, g, x, m))


def pick(t_ref, own_ref, peer_ref, j, half):
    h, at = divmod(j, half)
    cols = slice(at * SIDE, (at + 1) * SIDE)
    return jnp.where(t_ref[0] == h, own_ref[:, cols], peer_ref[:, cols])


def select_kernel(t_ref, sel_ref, sec_ref, m_ref, own_ref, peer_ref, out_ref):
    blocks, kept = sec_ref.shape[:2]
    nrow, keep, ncol = out_ref.shape
    half = kept // 2
    lane = lax.broadcasted_iota(jnp.int32, (nrow * keep, LANES), 1)
    acc = jnp.zeros((nrow * keep, LANES), f32)
    for j in range(blocks):
        x = pick(t_ref, own_ref, peer_ref, j, blocks // 2)
        parts = []
        for p in range(2):
            m = m_ref[p * LANES : (p + 1) * LANES, j * SIDE : (j + 1) * SIDE]
            r = mm(sel_ref[j, p], jnp.concatenate([m, x], axis=0))
            for n in range(0, half, ROWS):
                at = slice(0, LANES) if (n // ROWS) % 2 == 0 else slice(LANES, SIDE)
                parts.append(r[n : n + ROWS, at] + r[half + n : half + n + ROWS, at])
        r = jnp.concatenate(parts, axis=0) * sec_ref[j]
        total = jnp.broadcast_to(jnp.sum(r, axis=1, keepdims=True), r.shape)
        for c in range(GROUP):
            parts = [total[(i * GROUP + c) * keep : (i * GROUP + c + 1) * keep] for i in range(nrow)]
            acc = jnp.where(lane == j * GROUP + c, jnp.concatenate(parts, axis=0), acc)
    out_ref[...] = (acc * decay_rate)[:, :ncol].reshape(nrow, keep, ncol)


def select(t, sel, sec, m, own, peer, shape):
    return call(
        select_kernel,
        "select",
        flops=10**9,
        nbytes=6 * 10**6,
        in_specs=[SCALAR] + whole(5),
        out_specs=whole(1)[0],
        out_shape=VMEM(shape, f32),
    )(t, *vmem(sel, sec, m, own, peer))


def decoded(lt, sec, col):
    parts = split(sec * col)
    half = sec.shape[0] // 2
    none = jnp.zeros((ROWS, LANES), bf16)
    outs = []
    for p in range(2):
        wide = []
        for part in parts:
            at = [part[n : n + ROWS] for n in range(p * half, (p + 1) * half, ROWS)]
            left = [a if n % 2 == 0 else none for n, a in enumerate(at)]
            right = [none if n % 2 == 0 else a for n, a in enumerate(at)]
            wide.append(jnp.concatenate([jnp.concatenate(left, axis=0), jnp.concatenate(right, axis=0)], axis=1))
        hi, lo = wide
        rhs = jnp.concatenate([hi, hi, lo, jnp.zeros_like(lo)], axis=0)
        outs.append(mm(jnp.concatenate([lt[p], lt[p]], axis=1), rhs))
    return outs


def halves(t_ref, width, at, size):
    t = t_ref[0]
    mine = pl.ds(pl.multiple_of(t * width + at, LANES), size)
    theirs = pl.ds(pl.multiple_of((1 - t) * width + at, LANES), size)
    return mine, theirs


class Writer:
    def __init__(self, sems):
        self.sems, self.copies = sems, []

    def put(self, src, dst):
        copy = pltpu.make_async_copy(src, dst, self.sems.at[len(self.copies)])
        copy.start()
        self.copies.append(copy)

    def wait(self):
        for copy in self.copies:
            copy.wait()


STEP = 2
HEAD = 6
BODY = 12
CARRY = 2


def columns(start, stop):
    return pl.ds(start * SIDE, (stop - start) * SIDE)


def remain_block(refs, j, put):
    t_ref, lt_ref, sec_ref, gt_ref, m_ref, own_ref, peer_ref, c_ref = refs
    x = pick(t_ref, own_ref, peer_ref, j, lt_ref.shape[0] // 2)
    cols = slice(j * SIDE, (j + 1) * SIDE)
    grad = mm(gt_ref[...], x)
    less = decoded(lt_ref[j], sec_ref[j], column(-flat(c_ref), j))
    for p in range(2):
        at = slice(p * LANES, (p + 1) * LANES)
        moved = decay_rate * m_ref[at, cols].astype(f32) + grad[at]
        put(at, (moved + less[p]).astype(bf16))


def store_at(ref, n):
    def put(at, value):
        ref[at, n * SIDE : (n + 1) * SIDE] = value

    return put


def keys_kernel(*refs):
    *ins, w_ref, out_ref, part_ref, head_ref = refs
    t_ref, gt_ref, own_ref, peer_ref = ins[0], ins[3], ins[5], ins[6]
    width = own_ref.shape[1]
    mine, theirs = halves(t_ref, width, 0, width)
    away = w_ref[:, theirs]
    part_ref[:, :width] = away
    part_ref[:, width:] = gt_ref[...]
    out_ref[...] = (mm_t(w_ref[:, mine], own_ref[...]) + mm_t(away, peer_ref[...])).T.astype(bf16)
    for j in range(HEAD):
        remain_block(ins, j, store_at(head_ref, j))


def keys_of(t, lt, sec, gt, m, own, peer, c, w):
    return call(
        keys_kernel,
        "keys",
        flops=10**9,
        nbytes=4 * 10**6,
        in_specs=[SCALAR] + whole(8),
        out_specs=whole(3),
        out_shape=[
            VMEM((own.shape[0], w.shape[0]), bf16),
            VMEM((w.shape[0], own.shape[1] + gt.shape[1]), bf16),
            VMEM((m.shape[0], HEAD * SIDE), bf16),
        ],
    )(t, *vmem(lt, sec, gt, m, own, peer, c, w))


def remain_kernel(*refs):
    *ins, keys_ref, head_ref, keys_out, out_ref, carry_ref, buf, sems = refs
    writer = Writer(sems)
    writer.put(head_ref, out_ref.at[:, columns(0, HEAD)])
    writer.put(keys_ref, keys_out)
    stop = HEAD + BODY - CARRY
    begun = HEAD
    for j in range(HEAD, stop):
        remain_block(ins, j, store_at(buf, j))
        if (j + 1 - begun) == STEP or j + 1 == stop:
            at = columns(begun, j + 1)
            writer.put(buf.at[:, at], out_ref.at[:, at])
            begun = j + 1
    for n in range(CARRY):
        remain_block(ins, stop + n, store_at(carry_ref, n))
    writer.wait()


def remain(t, lt, sec, gt, m, own, peer, c, keys, head):
    return call(
        remain_kernel,
        "remain",
        flops=2 * 10**10,
        nbytes=8 * 10**6,
        in_specs=[SCALAR] + whole(9),
        out_specs=anywhere(2) + whole(1),
        out_shape=[
            jax.ShapeDtypeStruct(keys.shape, bf16),
            jax.ShapeDtypeStruct(m.shape, bf16),
            VMEM((m.shape[0], CARRY * SIDE), bf16),
        ],
        scratch_shapes=[pltpu.VMEM(m.shape, bf16), pltpu.SemaphoreType.DMA((BODY + 2,))],
    )(t, *vmem(lt, sec, gt, m, own, peer, c, keys, head))


def finish_kernel(*refs):
    *ins, carry_ref, g_ref, w_ref, dep_ref, begun_ref, out_ref, part_ref, buf, sems = refs
    t_ref = ins[0]
    blocks = ins[1].shape[0]
    start = HEAD + BODY
    writer = Writer(sems)
    writer.put(carry_ref, out_ref.at[:, columns(start - CARRY, start)])
    begun = start
    for j in range(start, blocks):
        remain_block(ins, j, store_at(buf, j))
        if (j + 1 - begun) == STEP or j + 1 == blocks:
            at = columns(begun, j + 1)
            writer.put(buf.at[:, at], out_ref.at[:, at])
            begun = j + 1
    width = part_ref.shape[1]
    for n in range(width // SIDE):
        mine, _ = halves(t_ref, width, n * SIDE, SIDE)
        part_ref[:, n * SIDE : (n + 1) * SIDE] = mm(g_ref[...], w_ref[:, mine])
    writer.wait()


def finish(begun, t, lt, sec, gt, m, own, peer, c, carry, g, w, dep):
    return call(
        finish_kernel,
        "finish",
        flops=10**9,
        nbytes=8 * 10**6,
        in_specs=[SCALAR] + whole(10) + anywhere(2),
        out_specs=anywhere(1) + whole(1),
        out_shape=[jax.ShapeDtypeStruct(m.shape, bf16), VMEM((g.shape[0], w.shape[1] // 2), f32)],
        scratch_shapes=[pltpu.VMEM(m.shape, bf16), pltpu.SemaphoreType.DMA((lt.shape[0],))],
        input_output_aliases={12: 0},
    )(t, *vmem(lt, sec, gt, m, own, peer, c, carry, g, w), dep, begun)


def update_kernel(scale, lt_ref, sec_ref, near_ref, far_ref, part_ref, wp_ref, out_ref, mean_ref, in_ref, buf, mean, in_buf, sems):
    blocks = lt_ref.shape[0]
    mean[...] = (near_ref[...] + far_ref[...]) * scale
    writer = Writer(sems)
    writer.put(mean, mean_ref)
    c = flat(mean)
    width = in_buf.shape[1]
    g = wp_ref[:, width:].T
    for n in range(width // SIDE):
        at = slice(n * SIDE, (n + 1) * SIDE)
        in_buf[:, at] = (part_ref[:, at] + mm(g, wp_ref[:, at])).astype(bf16)
        if n % STEP == STEP - 1:
            at = columns(n + 1 - STEP, n + 1)
            writer.put(in_buf.at[:, at], in_ref.at[:, at])
    begun = 0
    for j in range(blocks):
        out = decoded(lt_ref[j], sec_ref[j], column(c, j))
        for p in range(2):
            buf[p * LANES : (p + 1) * LANES, j * SIDE : (j + 1) * SIDE] = out[p].astype(bf16)
        if j == 0 or (j + 1 - begun) == STEP or j + 2 >= blocks:
            at = columns(begun, j + 1)
            writer.put(buf.at[:, at], out_ref.at[:, at])
            begun = j + 1
    writer.wait()


def update(lt, sec, near, far, part, wp, replicas, shape):
    blocks = lt.shape[0]
    assert blocks * SIDE == 2 * part.shape[1]
    return call(
        functools.partial(update_kernel, 1.0 / replicas),
        "update",
        flops=10**9,
        nbytes=6 * 10**6,
        in_specs=whole(6),
        out_specs=anywhere(3),
        out_shape=[
            jax.ShapeDtypeStruct(shape, bf16),
            jax.ShapeDtypeStruct(near.shape, f32),
            jax.ShapeDtypeStruct(part.shape, bf16),
        ],
        scratch_shapes=[
            pltpu.VMEM(shape, bf16),
            pltpu.VMEM(near.shape, f32),
            pltpu.VMEM(part.shape, bf16),
            pltpu.SemaphoreType.DMA((2 * blocks,)),
        ],
    )(*vmem(lt, sec, near, far, part, wp))


def shards(tokens, cotangent, key_weight, momentum, indices):
    replicas = lax.axis_size("replica")
    swap = [(0, 1), (1, 0)]
    t = lax.axis_index("tensor").astype(jnp.int32).reshape(1)
    peer = lax.ppermute(tokens, "tensor", swap)
    m = momentum[0]
    idx = indices.transpose(0, 2, 1)
    tab = jnp.asarray(dct_table())
    sel, sec, lt, gt, m_in, own = plan(idx, cotangent, tab, m, tokens)
    total = select(t, sel, sec, m_in, own, peer, idx.shape)
    mine = total

    rounds = replicas.bit_length() - 1

    def exchange(x, n):
        step = 1 << ((n + 1) % rounds)
        if rounds > 1 and n in (0, rounds - 1):
            pairs = [(2 * r + c, 2 * (r ^ step) + 1 - c) for r in range(replicas) for c in range(2)]
            return lax.ppermute(x, ("replica", "tensor"), pairs), lax.ppermute(x, "tensor", swap)
        return lax.ppermute(x, "replica", [(r, r ^ step) for r in range(replicas)]), x

    shared = (t, lt, sec, gt, m_in, own, peer, mine)
    far, near = exchange(total, 0)
    keys, w_part, head = keys_of(*shared, key_weight)
    total, keys, w_part = lax.optimization_barrier((near + far, keys, w_part))
    for n in range(1, rounds - 2):
        far, near = exchange(total, n)
        total = far + near
    far, near = exchange(total, rounds - 2)
    w_peer = lax.ppermute(w_part, "tensor", swap)
    keys, begun, carry = remain(*shared, keys, head)
    begun, total = lax.optimization_barrier((begun, near + far))
    far, near = exchange(total, rounds - 1)
    remaining, part = finish(begun, *shared, carry, cotangent, key_weight, total)
    remaining, near, far = lax.optimization_barrier((remaining, near, far))
    new_update, pooled, input_grad = update(lt, sec, near, far, part, w_peer, replicas, m.shape)
    return (keys, input_grad, remaining[None], new_update, pooled.transpose(0, 2, 1))


def solution(mesh):
    placed = (
        P(("groups", "replica"), "tensor"),
        P(("groups", "replica"), "tensor"),
        P("tensor", None),
        P(("groups", "replica"), "tensor", None),
        P("tensor", None, None),
    )
    return jax.shard_map(
        shards,
        mesh=mesh,
        in_specs=placed,
        out_specs=(
            P(("groups", "replica"), "tensor"),
            P(("groups", "replica"), "tensor"),
            P(("groups", "replica"), "tensor", None),
            P(("groups", "tensor"), None),
            P(("groups", "tensor"), None, None),
        ),
        check_vma=False,
    )
```

```python
import functools

import jax
import jax.numpy as jnp
import numpy as np
from jax import lax
from jax.experimental import pallas as pl
from jax.experimental.pallas import tpu as pltpu
from jax.sharding import PartitionSpec as P

SPAN = 64
GROUP = 4
SIDE = SPAN * GROUP
LANES = 128
ROWS = 16
decay_rate = 0.9
bf16 = jnp.bfloat16
f32 = jnp.float32
VMEM = pltpu.VMEM


def split(x):
    hi = x.astype(bf16)
    return hi, (x - hi.astype(f32)).astype(bf16)


def dct_table():
    freq = np.arange(SPAN, dtype=np.float64)[:, None]
    place = np.arange(SPAN, dtype=np.float64)[None, :]
    scale = np.where(freq == 0, np.sqrt(1.0 / SPAN), np.sqrt(2.0 / SPAN))
    table = scale * np.cos(np.pi * (2.0 * place + 1.0) * freq / (2.0 * SPAN))
    return np.tile(table, (1, LANES // SPAN)).astype(np.float32)


def mm(a, b):
    return jnp.dot(a, b, preferred_element_type=f32)


def mm_t(a, b):
    return lax.dot_general(a, b, (((1,), (1,)), ((), ())), preferred_element_type=f32)


def call(kernel, name, flops=0, nbytes=0, **kw):
    return pl.pallas_call(
        kernel,
        name=name,
        compiler_params=pltpu.CompilerParams(vmem_limit_bytes=16 * 2**20),
        cost_estimate=pl.CostEstimate(flops=flops, bytes_accessed=nbytes, transcendentals=0),
        **kw,
    )


def vmem(*xs):
    return [pltpu.with_memory_space_constraint(x, VMEM) for x in xs]


def hbm(*xs):
    return [pltpu.with_memory_space_constraint(x, pltpu.HBM) for x in xs]


def whole(n):
    return [pl.BlockSpec(memory_space=VMEM)] * n


def anywhere(n):
    return [pl.BlockSpec(memory_space=pl.ANY)] * n


SCALAR = pl.BlockSpec(memory_space=pltpu.SMEM)


def column(z, j):
    keep = z.shape[0] // GROUP
    parts = [
        jnp.broadcast_to(z[i * keep : (i + 1) * keep, c : c + 1], (keep, LANES))
        for i in range(GROUP)
        for c in range(j * GROUP, (j + 1) * GROUP)
    ]
    return jnp.concatenate(parts, axis=0)


def flat(ref):
    nrow, keep, ncol = ref.shape
    return ref[...].reshape(nrow * keep, ncol)


def plan_kernel(
    idx_hbm, tab_hbm, g_hbm, x_hbm, m_hbm, sel_ref, sec_ref, lt_ref, gt_ref, m_ref, x_ref, idx_ref, tab_ref, g_ref, sems
):
    pairs = ((idx_hbm, idx_ref), (tab_hbm, tab_ref), (g_hbm, g_ref), (x_hbm, x_ref), (m_hbm, m_ref))
    loads = [pltpu.make_async_copy(src, dst, sems.at[n]) for n, (src, dst) in enumerate(pairs)]
    for load in loads:
        load.start()
    for load in loads[:3]:
        load.wait()
    blocks, kept = sec_ref.shape[:2]
    per = kept // GROUP
    half = kept // 2
    z = flat(idx_ref)
    chi, clo = split(tab_ref[...])
    col_tab = jnp.concatenate([chi, clo], axis=0)
    none = jnp.zeros((LANES, LANES), bf16)
    col_tab = jnp.concatenate(
        [jnp.concatenate([col_tab, none], axis=1), jnp.concatenate([none, col_tab], axis=1)], axis=0
    )
    lane = lax.broadcasted_iota(jnp.int32, (kept, LANES), 1)
    row = lax.broadcasted_iota(jnp.int32, (kept, LANES), 0)
    place = lane - SPAN * ((row // per) & 1)
    lane_in = lane & (SPAN - 1)
    mine = (lane // SPAN) == ((row // (per // GROUP)) & 1)
    hi = jnp.concatenate([chi, chi], axis=0)
    lo = jnp.concatenate([clo, clo], axis=0)
    near = lax.broadcasted_iota(jnp.int32, hi.shape, 0) // SPAN == lax.broadcasted_iota(jnp.int32, hi.shape, 1) // SPAN
    hi = jnp.where(near, hi, jnp.zeros_like(hi))
    lo = jnp.where(near, lo, jnp.zeros_like(lo))
    g = g_ref[...]
    row_g = [mm_t(hi, g[:, at : at + LANES]) + mm_t(lo, g[:, at : at + LANES]) for at in range(0, SIDE, LANES)]
    ghi, glo = split(jnp.concatenate(row_g, axis=0) * (1.0 / decay_rate))
    hi, lo = [jnp.concatenate([part, part], axis=0) for part in (hi, lo)]
    row_tab = jnp.concatenate([hi, ghi, lo, glo], axis=1)
    none = jnp.zeros((half, LANES), bf16)
    group = 10
    for j in range(0, blocks, group):
        cols = [column(z, k) for k in range(j, j + group)]
        one_b = [jnp.where((col & (SPAN - 1)) == lane_in, 1.0, 0.0).astype(bf16) for col in cols]
        one_a = []
        for col in cols:
            one = jnp.where((col >> 6) == place, 1.0, 0.0).astype(bf16)
            one_a.append(jnp.concatenate([one[:half], none], axis=1))
            one_a.append(jnp.concatenate([none, one[half:]], axis=1))
        pairs = [jnp.concatenate(one_b[k : k + 2], axis=1) for k in range(0, group, 2)]
        sec = mm(jnp.concatenate(pairs, axis=0), col_tab)
        rows = mm(jnp.concatenate(one_a, axis=0), row_tab).astype(bf16)
        for k in range(group):
            sec_ref[j + k] = jnp.where(mine, sec[k // 2 * kept : (k // 2 + 1) * kept, k % 2 * LANES : (k % 2 + 1) * LANES], 0.0)
            for p in range(2):
                at = slice(k * kept + p * half, k * kept + (p + 1) * half)
                sel_ref[j + k, p, :half, :] = rows[at, :SIDE]
                sel_ref[j + k, p, half:, :] = rows[at, SIDE:]
                lt_ref[j + k, p] = jnp.concatenate([rows[at, :LANES], rows[at, SIDE : SIDE + LANES]], axis=0).T
    gt_ref[...] = g.T
    for load in loads[3:]:
        load.wait()


def plan(idx, g, tab, m, x):
    nrow, keep, ncol = idx.shape
    blocks, kept = ncol // GROUP, GROUP * GROUP * keep
    tok = g.shape[0]
    return call(
        plan_kernel,
        "plan",
        flops=2 * 10**9,
        nbytes=4 * 10**6,
        in_specs=anywhere(5),
        out_specs=whole(6),
        out_shape=[
            VMEM((blocks, 2, kept, LANES + tok), bf16),
            VMEM((blocks, kept, LANES), f32),
            VMEM((blocks, 2, LANES, kept), bf16),
            VMEM((g.shape[1], tok), bf16),
            VMEM(m.shape, bf16),
            VMEM(x.shape, bf16),
        ],
        scratch_shapes=[
            pltpu.VMEM(idx.shape, jnp.int32),
            pltpu.VMEM(tab.shape, f32),
            pltpu.VMEM(g.shape, bf16),
            pltpu.SemaphoreType.DMA((5,)),
        ],
    )(*hbm(idx, tab, g, x, m))


def pick(t_ref, own_ref, peer_ref, j, half):
    h, at = divmod(j, half)
    cols = slice(at * SIDE, (at + 1) * SIDE)
    return jnp.where(t_ref[0] == h, own_ref[:, cols], peer_ref[:, cols])


def select_kernel(t_ref, sel_ref, sec_ref, m_ref, own_ref, peer_ref, out_ref):
    blocks, kept = sec_ref.shape[:2]
    nrow, keep, ncol = out_ref.shape
    half = kept // 2
    lane = lax.broadcasted_iota(jnp.int32, (nrow * keep, LANES), 1)
    acc = jnp.zeros((nrow * keep, LANES), f32)
    for j in range(blocks):
        x = pick(t_ref, own_ref, peer_ref, j, blocks // 2)
        parts = []
        for p in range(2):
            m = m_ref[p * LANES : (p + 1) * LANES, j * SIDE : (j + 1) * SIDE]
            r = mm(sel_ref[j, p], jnp.concatenate([m, x], axis=0))
            for n in range(0, half, ROWS):
                at = slice(0, LANES) if (n // ROWS) % 2 == 0 else slice(LANES, SIDE)
                parts.append(r[n : n + ROWS, at] + r[half + n : half + n + ROWS, at])
        r = jnp.concatenate(parts, axis=0) * sec_ref[j]
        total = jnp.broadcast_to(jnp.sum(r, axis=1, keepdims=True), r.shape)
        for c in range(GROUP):
            parts = [total[(i * GROUP + c) * keep : (i * GROUP + c + 1) * keep] for i in range(nrow)]
            acc = jnp.where(lane == j * GROUP + c, jnp.concatenate(parts, axis=0), acc)
    out_ref[...] = (acc * decay_rate)[:, :ncol].reshape(nrow, keep, ncol)


def select(t, sel, sec, m, own, peer, shape):
    return call(
        select_kernel,
        "select",
        flops=10**9,
        nbytes=6 * 10**6,
        in_specs=[SCALAR] + whole(5),
        out_specs=whole(1)[0],
        out_shape=VMEM(shape, f32),
    )(t, *vmem(sel, sec, m, own, peer))


def decoded(lt, sec, col):
    parts = split(sec * col)
    half = sec.shape[0] // 2
    none = jnp.zeros((ROWS, LANES), bf16)
    outs = []
    for p in range(2):
        wide = []
        for part in parts:
            at = [part[n : n + ROWS] for n in range(p * half, (p + 1) * half, ROWS)]
            left = [a if n % 2 == 0 else none for n, a in enumerate(at)]
            right = [none if n % 2 == 0 else a for n, a in enumerate(at)]
            wide.append(jnp.concatenate([jnp.concatenate(left, axis=0), jnp.concatenate(right, axis=0)], axis=1))
        hi, lo = wide
        rhs = jnp.concatenate([hi, hi, lo, jnp.zeros_like(lo)], axis=0)
        outs.append(mm(jnp.concatenate([lt[p], lt[p]], axis=1), rhs))
    return outs


def halves(t_ref, width, at, size):
    t = t_ref[0]
    mine = pl.ds(pl.multiple_of(t * width + at, LANES), size)
    theirs = pl.ds(pl.multiple_of((1 - t) * width + at, LANES), size)
    return mine, theirs


class Writer:
    def __init__(self, sems):
        self.sems, self.copies = sems, []

    def put(self, src, dst):
        copy = pltpu.make_async_copy(src, dst, self.sems.at[len(self.copies)])
        copy.start()
        self.copies.append(copy)

    def wait(self):
        for copy in self.copies:
            copy.wait()


STEP = 1
HEAD = 6
BODY = 12
CARRY = 2


def columns(start, stop):
    return pl.ds(start * SIDE, (stop - start) * SIDE)


def remain_block(refs, j, put):
    t_ref, lt_ref, sec_ref, gt_ref, m_ref, own_ref, peer_ref, c_ref = refs
    x = pick(t_ref, own_ref, peer_ref, j, lt_ref.shape[0] // 2)
    cols = slice(j * SIDE, (j + 1) * SIDE)
    grad = mm(gt_ref[...], x)
    less = decoded(lt_ref[j], sec_ref[j], column(-flat(c_ref), j))
    for p in range(2):
        at = slice(p * LANES, (p + 1) * LANES)
        moved = decay_rate * m_ref[at, cols].astype(f32) + grad[at]
        put(at, (moved + less[p]).astype(bf16))


def store_at(ref, n):
    def put(at, value):
        ref[at, n * SIDE : (n + 1) * SIDE] = value

    return put


def keys_kernel(*refs):
    *ins, w_ref, out_ref, part_ref, head_ref = refs
    t_ref, gt_ref, own_ref, peer_ref = ins[0], ins[3], ins[5], ins[6]
    width = own_ref.shape[1]
    mine, theirs = halves(t_ref, width, 0, width)
    away = w_ref[:, theirs]
    part_ref[:, :width] = away
    part_ref[:, width:] = gt_ref[...]
    out_ref[...] = (mm_t(w_ref[:, mine], own_ref[...]) + mm_t(away, peer_ref[...])).T.astype(bf16)
    for j in range(HEAD):
        remain_block(ins, j, store_at(head_ref, j))


def keys_of(t, lt, sec, gt, m, own, peer, c, w):
    return call(
        keys_kernel,
        "keys",
        flops=10**9,
        nbytes=4 * 10**6,
        in_specs=[SCALAR] + whole(8),
        out_specs=whole(3),
        out_shape=[
            VMEM((own.shape[0], w.shape[0]), bf16),
            VMEM((w.shape[0], own.shape[1] + gt.shape[1]), bf16),
            VMEM((m.shape[0], HEAD * SIDE), bf16),
        ],
    )(t, *vmem(lt, sec, gt, m, own, peer, c, w))


def remain_kernel(*refs):
    *ins, keys_ref, head_ref, keys_out, out_ref, carry_ref, buf, sems = refs
    writer = Writer(sems)
    writer.put(head_ref, out_ref.at[:, columns(0, HEAD)])
    writer.put(keys_ref, keys_out)
    stop = HEAD + BODY - CARRY
    begun = HEAD
    for j in range(HEAD, stop):
        remain_block(ins, j, store_at(buf, j))
        if (j + 1 - begun) == STEP or j + 1 == stop:
            at = columns(begun, j + 1)
            writer.put(buf.at[:, at], out_ref.at[:, at])
            begun = j + 1
    for n in range(CARRY):
        remain_block(ins, stop + n, store_at(carry_ref, n))
    writer.wait()


def remain(t, lt, sec, gt, m, own, peer, c, keys, head):
    return call(
        remain_kernel,
        "remain",
        flops=2 * 10**10,
        nbytes=8 * 10**6,
        in_specs=[SCALAR] + whole(9),
        out_specs=anywhere(2) + whole(1),
        out_shape=[
            jax.ShapeDtypeStruct(keys.shape, bf16),
            jax.ShapeDtypeStruct(m.shape, bf16),
            VMEM((m.shape[0], CARRY * SIDE), bf16),
        ],
        scratch_shapes=[pltpu.VMEM(m.shape, bf16), pltpu.SemaphoreType.DMA((BODY + 2,))],
    )(t, *vmem(lt, sec, gt, m, own, peer, c, keys, head))


def finish_kernel(*refs):
    *ins, carry_ref, g_ref, w_ref, dep_ref, begun_ref, out_ref, part_ref, buf, sems = refs
    t_ref = ins[0]
    blocks = ins[1].shape[0]
    start = HEAD + BODY
    writer = Writer(sems)
    writer.put(carry_ref, out_ref.at[:, columns(start - CARRY, start)])
    begun = start
    for j in range(start, blocks):
        remain_block(ins, j, store_at(buf, j))
        if (j + 1 - begun) == STEP or j + 1 == blocks:
            at = columns(begun, j + 1)
            writer.put(buf.at[:, at], out_ref.at[:, at])
            begun = j + 1
    width = part_ref.shape[1]
    for n in range(width // SIDE):
        mine, _ = halves(t_ref, width, n * SIDE, SIDE)
        part_ref[:, n * SIDE : (n + 1) * SIDE] = mm(g_ref[...], w_ref[:, mine])
    writer.wait()


def finish(begun, t, lt, sec, gt, m, own, peer, c, carry, g, w, dep):
    return call(
        finish_kernel,
        "finish",
        flops=10**9,
        nbytes=8 * 10**6,
        in_specs=[SCALAR] + whole(10) + anywhere(2),
        out_specs=anywhere(1) + whole(1),
        out_shape=[jax.ShapeDtypeStruct(m.shape, bf16), VMEM((g.shape[0], w.shape[1] // 2), f32)],
        scratch_shapes=[pltpu.VMEM(m.shape, bf16), pltpu.SemaphoreType.DMA((lt.shape[0],))],
        input_output_aliases={12: 0},
    )(t, *vmem(lt, sec, gt, m, own, peer, c, carry, g, w), dep, begun)


def update_kernel(scale, lt_ref, sec_ref, sum_ref, part_ref, wp_ref, out_ref, mean_ref, in_ref, buf, mean, in_buf, sems):
    blocks = lt_ref.shape[0]
    mean[...] = sum_ref[...] * scale
    writer = Writer(sems)
    writer.put(mean, mean_ref)
    c = flat(mean)
    width = in_buf.shape[1]
    g = wp_ref[:, width:].T
    for n in range(width // SIDE):
        at = slice(n * SIDE, (n + 1) * SIDE)
        in_buf[:, at] = (part_ref[:, at] + mm(g, wp_ref[:, at])).astype(bf16)
        if n % STEP == STEP - 1:
            at = columns(n + 1 - STEP, n + 1)
            writer.put(in_buf.at[:, at], in_ref.at[:, at])
    begun = 0
    for j in range(blocks):
        out = decoded(lt_ref[j], sec_ref[j], column(c, j))
        for p in range(2):
            buf[p * LANES : (p + 1) * LANES, j * SIDE : (j + 1) * SIDE] = out[p].astype(bf16)
        if j == 0 or (j + 1 - begun) == STEP or j + 2 >= blocks:
            at = columns(begun, j + 1)
            writer.put(buf.at[:, at], out_ref.at[:, at])
            begun = j + 1
    writer.wait()


def update(lt, sec, total, part, wp, replicas, shape):
    blocks = lt.shape[0]
    assert blocks * SIDE == 2 * part.shape[1]
    return call(
        functools.partial(update_kernel, 1.0 / replicas),
        "update",
        flops=10**9,
        nbytes=6 * 10**6,
        in_specs=whole(5),
        out_specs=anywhere(3),
        out_shape=[
            jax.ShapeDtypeStruct(shape, bf16),
            jax.ShapeDtypeStruct(total.shape, f32),
            jax.ShapeDtypeStruct(part.shape, bf16),
        ],
        scratch_shapes=[
            pltpu.VMEM(shape, bf16),
            pltpu.VMEM(total.shape, f32),
            pltpu.VMEM(part.shape, bf16),
            pltpu.SemaphoreType.DMA((2 * blocks,)),
        ],
    )(*vmem(lt, sec, total, part, wp))


def shards(tokens, cotangent, key_weight, momentum, indices):
    replicas = lax.axis_size("replica")
    swap = [(0, 1), (1, 0)]
    t = lax.axis_index("tensor").astype(jnp.int32).reshape(1)
    peer = lax.ppermute(tokens, "tensor", swap)
    m = momentum[0]
    idx = indices.transpose(0, 2, 1)
    tab = jnp.asarray(dct_table())
    sel, sec, lt, gt, m_in, own = plan(idx, cotangent, tab, m, tokens)
    total = select(t, sel, sec, m_in, own, peer, idx.shape)
    mine = total

    rounds = replicas.bit_length() - 1

    def exchange(x, n):
        step = 1 << n
        if rounds > 1 and n in (0, rounds - 1):
            pairs = [(2 * r + c, 2 * (r ^ step) + 1 - c) for r in range(replicas) for c in range(2)]
            return lax.ppermute(x, ("replica", "tensor"), pairs), lax.ppermute(x, "tensor", swap)
        return lax.ppermute(x, "replica", [(r, r ^ step) for r in range(replicas)]), x

    shared = (t, lt, sec, gt, m_in, own, peer, mine)
    far, near = exchange(total, 0)
    keys, w_part, head = keys_of(*shared, key_weight)
    total, keys, w_part = lax.optimization_barrier((near + far, keys, w_part))
    for n in range(1, rounds - 2):
        far, near = exchange(total, n)
        total = far + near
    far, near = exchange(total, rounds - 2)
    w_peer = lax.ppermute(w_part, "tensor", swap)
    keys, begun, carry = remain(*shared, keys, head)
    begun, total = lax.optimization_barrier((begun, near + far))
    far, near = exchange(total, rounds - 1)
    remaining, part = finish(begun, *shared, carry, cotangent, key_weight, total)
    remaining, total = lax.optimization_barrier((remaining, near + far))
    new_update, pooled, input_grad = update(lt, sec, total, part, w_peer, replicas, m.shape)
    return (keys, input_grad, remaining[None], new_update, pooled.transpose(0, 2, 1))


def solution(mesh):
    placed = (
        P(("groups", "replica"), "tensor"),
        P(("groups", "replica"), "tensor"),
        P("tensor", None),
        P(("groups", "replica"), "tensor", None),
        P("tensor", None, None),
    )
    return jax.shard_map(
        shards,
        mesh=mesh,
        in_specs=placed,
        out_specs=(
            P(("groups", "replica"), "tensor"),
            P(("groups", "replica"), "tensor"),
            P(("groups", "replica"), "tensor", None),
            P(("groups", "tensor"), None),
            P(("groups", "tensor"), None, None),
        ),
        check_vma=False,
    )
```

```python
import functools

import jax
import jax.numpy as jnp
import numpy as np
from jax import lax
from jax.experimental import pallas as pl
from jax.experimental.pallas import tpu as pltpu
from jax.sharding import PartitionSpec as P

SPAN = 64
GROUP = 4
SIDE = SPAN * GROUP
LANES = 128
ROWS = 16
decay_rate = 0.9
bf16 = jnp.bfloat16
f32 = jnp.float32
VMEM = pltpu.VMEM


def split(x):
    hi = x.astype(bf16)
    return hi, (x - hi.astype(f32)).astype(bf16)


def dct_table():
    freq = np.arange(SPAN, dtype=np.float64)[:, None]
    place = np.arange(SPAN, dtype=np.float64)[None, :]
    scale = np.where(freq == 0, np.sqrt(1.0 / SPAN), np.sqrt(2.0 / SPAN))
    table = scale * np.cos(np.pi * (2.0 * place + 1.0) * freq / (2.0 * SPAN))
    return np.tile(table, (1, LANES // SPAN)).astype(np.float32)


def mm(a, b):
    return jnp.dot(a, b, preferred_element_type=f32)


def mm_t(a, b):
    return lax.dot_general(a, b, (((1,), (1,)), ((), ())), preferred_element_type=f32)


def call(kernel, name, flops=0, nbytes=0, **kw):
    return pl.pallas_call(
        kernel,
        name=name,
        compiler_params=pltpu.CompilerParams(vmem_limit_bytes=16 * 2**20),
        cost_estimate=pl.CostEstimate(flops=flops, bytes_accessed=nbytes, transcendentals=0),
        **kw,
    )


def vmem(*xs):
    return [pltpu.with_memory_space_constraint(x, VMEM) for x in xs]


def hbm(*xs):
    return [pltpu.with_memory_space_constraint(x, pltpu.HBM) for x in xs]


def whole(n):
    return [pl.BlockSpec(memory_space=VMEM)] * n


def anywhere(n):
    return [pl.BlockSpec(memory_space=pl.ANY)] * n


SCALAR = pl.BlockSpec(memory_space=pltpu.SMEM)


def column(z, j):
    keep = z.shape[0] // GROUP
    parts = [
        jnp.broadcast_to(z[i * keep : (i + 1) * keep, c : c + 1], (keep, LANES))
        for i in range(GROUP)
        for c in range(j * GROUP, (j + 1) * GROUP)
    ]
    return jnp.concatenate(parts, axis=0)


def flat(ref):
    nrow, keep, ncol = ref.shape
    return ref[...].reshape(nrow * keep, ncol)


def plan_kernel(
    idx_hbm, tab_hbm, g_hbm, x_hbm, m_hbm, sel_ref, sec_ref, lt_ref, gt_ref, m_ref, x_ref, idx_ref, tab_ref, g_ref, sems
):
    pairs = ((idx_hbm, idx_ref), (tab_hbm, tab_ref), (g_hbm, g_ref), (x_hbm, x_ref), (m_hbm, m_ref))
    loads = [pltpu.make_async_copy(src, dst, sems.at[n]) for n, (src, dst) in enumerate(pairs)]
    for load in loads:
        load.start()
    for load in loads[:3]:
        load.wait()
    blocks, kept = sec_ref.shape[:2]
    per = kept // GROUP
    half = kept // 2
    z = flat(idx_ref)
    chi, clo = split(tab_ref[...])
    col_tab = jnp.concatenate([chi, clo], axis=0)
    none = jnp.zeros((LANES, LANES), bf16)
    col_tab = jnp.concatenate(
        [jnp.concatenate([col_tab, none], axis=1), jnp.concatenate([none, col_tab], axis=1)], axis=0
    )
    lane = lax.broadcasted_iota(jnp.int32, (kept, LANES), 1)
    row = lax.broadcasted_iota(jnp.int32, (kept, LANES), 0)
    place = lane - SPAN * ((row // per) & 1)
    lane_in = lane & (SPAN - 1)
    mine = (lane // SPAN) == ((row // (per // GROUP)) & 1)
    hi = jnp.concatenate([chi, chi], axis=0)
    lo = jnp.concatenate([clo, clo], axis=0)
    near = lax.broadcasted_iota(jnp.int32, hi.shape, 0) // SPAN == lax.broadcasted_iota(jnp.int32, hi.shape, 1) // SPAN
    hi = jnp.where(near, hi, jnp.zeros_like(hi))
    lo = jnp.where(near, lo, jnp.zeros_like(lo))
    g = g_ref[...]
    row_g = [mm_t(hi, g[:, at : at + LANES]) + mm_t(lo, g[:, at : at + LANES]) for at in range(0, SIDE, LANES)]
    ghi, glo = split(jnp.concatenate(row_g, axis=0) * (1.0 / decay_rate))
    hi, lo = [jnp.concatenate([part, part], axis=0) for part in (hi, lo)]
    row_tab = jnp.concatenate([hi, ghi, lo, glo], axis=1)
    none = jnp.zeros((half, LANES), bf16)
    group = 10
    for j in range(0, blocks, group):
        cols = [column(z, k) for k in range(j, j + group)]
        one_b = [jnp.where((col & (SPAN - 1)) == lane_in, 1.0, 0.0).astype(bf16) for col in cols]
        one_a = []
        for col in cols:
            one = jnp.where((col >> 6) == place, 1.0, 0.0).astype(bf16)
            one_a.append(jnp.concatenate([one[:half], none], axis=1))
            one_a.append(jnp.concatenate([none, one[half:]], axis=1))
        pairs = [jnp.concatenate(one_b[k : k + 2], axis=1) for k in range(0, group, 2)]
        sec = mm(jnp.concatenate(pairs, axis=0), col_tab)
        rows = mm(jnp.concatenate(one_a, axis=0), row_tab).astype(bf16)
        for k in range(group):
            sec_ref[j + k] = jnp.where(mine, sec[k // 2 * kept : (k // 2 + 1) * kept, k % 2 * LANES : (k % 2 + 1) * LANES], 0.0)
            for p in range(2):
                at = slice(k * kept + p * half, k * kept + (p + 1) * half)
                sel_ref[j + k, p, :half, :] = rows[at, :SIDE]
                sel_ref[j + k, p, half:, :] = rows[at, SIDE:]
                lt_ref[j + k, p] = jnp.concatenate([rows[at, :LANES], rows[at, SIDE : SIDE + LANES]], axis=0).T
    gt_ref[...] = g.T
    for load in loads[3:]:
        load.wait()


def plan(idx, g, tab, m, x):
    nrow, keep, ncol = idx.shape
    blocks, kept = ncol // GROUP, GROUP * GROUP * keep
    tok = g.shape[0]
    return call(
        plan_kernel,
        "plan",
        flops=2 * 10**9,
        nbytes=4 * 10**6,
        in_specs=anywhere(5),
        out_specs=whole(6),
        out_shape=[
            VMEM((blocks, 2, kept, LANES + tok), bf16),
            VMEM((blocks, kept, LANES), f32),
            VMEM((blocks, 2, LANES, kept), bf16),
            VMEM((g.shape[1], tok), bf16),
            VMEM(m.shape, bf16),
            VMEM(x.shape, bf16),
        ],
        scratch_shapes=[
            pltpu.VMEM(idx.shape, jnp.int32),
            pltpu.VMEM(tab.shape, f32),
            pltpu.VMEM(g.shape, bf16),
            pltpu.SemaphoreType.DMA((5,)),
        ],
    )(*hbm(idx, tab, g, x, m))


def pick(t_ref, own_ref, peer_ref, j, half):
    h, at = divmod(j, half)
    cols = slice(at * SIDE, (at + 1) * SIDE)
    return jnp.where(t_ref[0] == h, own_ref[:, cols], peer_ref[:, cols])


def select_kernel(t_ref, sel_ref, sec_ref, m_ref, own_ref, peer_ref, out_ref):
    blocks, kept = sec_ref.shape[:2]
    nrow, keep, ncol = out_ref.shape
    half = kept // 2
    lane = lax.broadcasted_iota(jnp.int32, (nrow * keep, LANES), 1)
    acc = jnp.zeros((nrow * keep, LANES), f32)
    for j in range(blocks):
        x = pick(t_ref, own_ref, peer_ref, j, blocks // 2)
        parts = []
        for p in range(2):
            m = m_ref[p * LANES : (p + 1) * LANES, j * SIDE : (j + 1) * SIDE]
            r = mm(sel_ref[j, p], jnp.concatenate([m, x], axis=0))
            for n in range(0, half, ROWS):
                at = slice(0, LANES) if (n // ROWS) % 2 == 0 else slice(LANES, SIDE)
                parts.append(r[n : n + ROWS, at] + r[half + n : half + n + ROWS, at])
        r = jnp.concatenate(parts, axis=0) * sec_ref[j]
        total = jnp.broadcast_to(jnp.sum(r, axis=1, keepdims=True), r.shape)
        for c in range(GROUP):
            parts = [total[(i * GROUP + c) * keep : (i * GROUP + c + 1) * keep] for i in range(nrow)]
            acc = jnp.where(lane == j * GROUP + c, jnp.concatenate(parts, axis=0), acc)
    out_ref[...] = (acc * decay_rate)[:, :ncol].reshape(nrow, keep, ncol)


def select(t, sel, sec, m, own, peer, shape):
    return call(
        select_kernel,
        "select",
        flops=10**9,
        nbytes=6 * 10**6,
        in_specs=[SCALAR] + whole(5),
        out_specs=whole(1)[0],
        out_shape=VMEM(shape, f32),
    )(t, *vmem(sel, sec, m, own, peer))


def decoded(lt, sec, col):
    parts = split(sec * col)
    half = sec.shape[0] // 2
    none = jnp.zeros((ROWS, LANES), bf16)
    outs = []
    for p in range(2):
        wide = []
        for part in parts:
            at = [part[n : n + ROWS] for n in range(p * half, (p + 1) * half, ROWS)]
            left = [a if n % 2 == 0 else none for n, a in enumerate(at)]
            right = [none if n % 2 == 0 else a for n, a in enumerate(at)]
            wide.append(jnp.concatenate([jnp.concatenate(left, axis=0), jnp.concatenate(right, axis=0)], axis=1))
        hi, lo = wide
        rhs = jnp.concatenate([hi, hi, lo, jnp.zeros_like(lo)], axis=0)
        outs.append(mm(jnp.concatenate([lt[p], lt[p]], axis=1), rhs))
    return outs


def halves(t_ref, width, at, size):
    t = t_ref[0]
    mine = pl.ds(pl.multiple_of(t * width + at, LANES), size)
    theirs = pl.ds(pl.multiple_of((1 - t) * width + at, LANES), size)
    return mine, theirs


class Writer:
    def __init__(self, sems):
        self.sems, self.copies = sems, []

    def put(self, src, dst):
        copy = pltpu.make_async_copy(src, dst, self.sems.at[len(self.copies)])
        copy.start()
        self.copies.append(copy)

    def wait(self):
        for copy in self.copies:
            copy.wait()


STEP = 2
HEAD = 6
BODY = 12
CARRY = 2


def columns(start, stop):
    return pl.ds(start * SIDE, (stop - start) * SIDE)


def remain_block(refs, j, put):
    t_ref, lt_ref, sec_ref, gt_ref, m_ref, own_ref, peer_ref, c_ref = refs
    x = pick(t_ref, own_ref, peer_ref, j, lt_ref.shape[0] // 2)
    cols = slice(j * SIDE, (j + 1) * SIDE)
    grad = mm(gt_ref[...], x)
    less = decoded(lt_ref[j], sec_ref[j], column(-flat(c_ref), j))
    for p in range(2):
        at = slice(p * LANES, (p + 1) * LANES)
        moved = decay_rate * m_ref[at, cols].astype(f32) + grad[at]
        put(at, (moved + less[p]).astype(bf16))


def store_at(ref, n):
    def put(at, value):
        ref[at, n * SIDE : (n + 1) * SIDE] = value

    return put


def keys_kernel(*refs):
    *ins, w_ref, out_ref, part_ref, head_ref = refs
    t_ref, gt_ref, own_ref, peer_ref = ins[0], ins[3], ins[5], ins[6]
    width = own_ref.shape[1]
    mine, theirs = halves(t_ref, width, 0, width)
    away = w_ref[:, theirs]
    part_ref[:, :width] = away
    part_ref[:, width:] = gt_ref[...]
    out_ref[...] = (mm_t(w_ref[:, mine], own_ref[...]) + mm_t(away, peer_ref[...])).T.astype(bf16)
    for j in range(HEAD):
        remain_block(ins, j, store_at(head_ref, j))


def keys_of(t, lt, sec, gt, m, own, peer, c, w):
    return call(
        keys_kernel,
        "keys",
        flops=10**9,
        nbytes=4 * 10**6,
        in_specs=[SCALAR] + whole(8),
        out_specs=whole(3),
        out_shape=[
            VMEM((own.shape[0], w.shape[0]), bf16),
            VMEM((w.shape[0], own.shape[1] + gt.shape[1]), bf16),
            VMEM((m.shape[0], HEAD * SIDE), bf16),
        ],
    )(t, *vmem(lt, sec, gt, m, own, peer, c, w))


def remain_kernel(*refs):
    *ins, keys_ref, head_ref, keys_out, out_ref, carry_ref, buf, sems = refs
    writer = Writer(sems)
    writer.put(head_ref, out_ref.at[:, columns(0, HEAD)])
    writer.put(keys_ref, keys_out)
    stop = HEAD + BODY - CARRY
    begun = HEAD
    for j in range(HEAD, stop):
        remain_block(ins, j, store_at(buf, j))
        if (j + 1 - begun) == STEP or j + 1 == stop:
            at = columns(begun, j + 1)
            writer.put(buf.at[:, at], out_ref.at[:, at])
            begun = j + 1
    for n in range(CARRY):
        remain_block(ins, stop + n, store_at(carry_ref, n))
    writer.wait()


def remain(t, lt, sec, gt, m, own, peer, c, keys, head):
    return call(
        remain_kernel,
        "remain",
        flops=2 * 10**10,
        nbytes=8 * 10**6,
        in_specs=[SCALAR] + whole(9),
        out_specs=anywhere(2) + whole(1),
        out_shape=[
            jax.ShapeDtypeStruct(keys.shape, bf16),
            jax.ShapeDtypeStruct(m.shape, bf16),
            VMEM((m.shape[0], CARRY * SIDE), bf16),
        ],
        scratch_shapes=[pltpu.VMEM(m.shape, bf16), pltpu.SemaphoreType.DMA((BODY + 2,))],
    )(t, *vmem(lt, sec, gt, m, own, peer, c, keys, head))


def finish_kernel(*refs):
    *ins, carry_ref, g_ref, w_ref, dep_ref, begun_ref, out_ref, part_ref, buf, sems = refs
    t_ref = ins[0]
    blocks = ins[1].shape[0]
    start = HEAD + BODY
    writer = Writer(sems)
    writer.put(carry_ref, out_ref.at[:, columns(start - CARRY, start)])
    begun = start
    for j in range(start, blocks):
        remain_block(ins, j, store_at(buf, j))
        if (j + 1 - begun) == STEP or j + 1 == blocks:
            at = columns(begun, j + 1)
            writer.put(buf.at[:, at], out_ref.at[:, at])
            begun = j + 1
    width = part_ref.shape[1]
    for n in range(width // SIDE):
        mine, _ = halves(t_ref, width, n * SIDE, SIDE)
        part_ref[:, n * SIDE : (n + 1) * SIDE] = mm(g_ref[...], w_ref[:, mine])
    writer.wait()


def finish(begun, t, lt, sec, gt, m, own, peer, c, carry, g, w, dep):
    return call(
        finish_kernel,
        "finish",
        flops=10**9,
        nbytes=8 * 10**6,
        in_specs=[SCALAR] + whole(10) + anywhere(2),
        out_specs=anywhere(1) + whole(1),
        out_shape=[jax.ShapeDtypeStruct(m.shape, bf16), VMEM((g.shape[0], w.shape[1] // 2), f32)],
        scratch_shapes=[pltpu.VMEM(m.shape, bf16), pltpu.SemaphoreType.DMA((lt.shape[0],))],
        input_output_aliases={12: 0},
    )(t, *vmem(lt, sec, gt, m, own, peer, c, carry, g, w), dep, begun)


def update_kernel(scale, lt_ref, sec_ref, near_ref, far_ref, part_ref, wp_ref, out_ref, mean_ref, in_ref, buf, mean, in_buf, sems):
    blocks = lt_ref.shape[0]
    mean[...] = (near_ref[...] + far_ref[...]) * scale
    writer = Writer(sems)
    writer.put(mean, mean_ref)
    c = flat(mean)
    width = in_buf.shape[1]
    g = wp_ref[:, width:].T
    for n in range(width // SIDE):
        at = slice(n * SIDE, (n + 1) * SIDE)
        in_buf[:, at] = (part_ref[:, at] + mm(g, wp_ref[:, at])).astype(bf16)
        if n % STEP == STEP - 1:
            at = columns(n + 1 - STEP, n + 1)
            writer.put(in_buf.at[:, at], in_ref.at[:, at])
    begun = 0
    for j in range(blocks):
        out = decoded(lt_ref[j], sec_ref[j], column(c, j))
        for p in range(2):
            buf[p * LANES : (p + 1) * LANES, j * SIDE : (j + 1) * SIDE] = out[p].astype(bf16)
        if j == 0 or (j + 1 - begun) == STEP or j + 2 >= blocks:
            at = columns(begun, j + 1)
            writer.put(buf.at[:, at], out_ref.at[:, at])
            begun = j + 1
    writer.wait()


def update(lt, sec, near, far, part, wp, replicas, shape):
    blocks = lt.shape[0]
    assert blocks * SIDE == 2 * part.shape[1]
    return call(
        functools.partial(update_kernel, 1.0 / replicas),
        "update",
        flops=10**9,
        nbytes=6 * 10**6,
        in_specs=whole(6),
        out_specs=anywhere(3),
        out_shape=[
            jax.ShapeDtypeStruct(shape, bf16),
            jax.ShapeDtypeStruct(near.shape, f32),
            jax.ShapeDtypeStruct(part.shape, bf16),
        ],
        scratch_shapes=[
            pltpu.VMEM(shape, bf16),
            pltpu.VMEM(near.shape, f32),
            pltpu.VMEM(part.shape, bf16),
            pltpu.SemaphoreType.DMA((2 * blocks,)),
        ],
    )(*vmem(lt, sec, near, far, part, wp))


def shards(tokens, cotangent, key_weight, momentum, indices):
    replicas = lax.axis_size("replica")
    swap = [(0, 1), (1, 0)]
    t = lax.axis_index("tensor").astype(jnp.int32).reshape(1)
    peer = lax.ppermute(tokens, "tensor", swap)
    m = momentum[0]
    idx = indices.transpose(0, 2, 1)
    tab = jnp.asarray(dct_table())
    sel, sec, lt, gt, m_in, own = plan(idx, cotangent, tab, m, tokens)
    total = select(t, sel, sec, m_in, own, peer, idx.shape)
    mine = total

    rounds = replicas.bit_length() - 1

    def exchange(x, n):
        step = 1 << n
        if rounds > 1 and n in (0, rounds - 1):
            pairs = [(2 * r + c, 2 * (r ^ step) + 1 - c) for r in range(replicas) for c in range(2)]
            return lax.ppermute(x, ("replica", "tensor"), pairs), lax.ppermute(x, "tensor", swap)
        return lax.ppermute(x, "replica", [(r, r ^ step) for r in range(replicas)]), x

    shared = (t, lt, sec, gt, m_in, own, peer, mine)
    far, near = exchange(total, 0)
    keys, w_part, head = keys_of(*shared, key_weight)
    total, keys, w_part = lax.optimization_barrier((near + far, keys, w_part))
    for n in range(1, rounds - 2):
        far, near = exchange(total, n)
        total = far + near
    far, near = exchange(total, rounds - 2)
    w_peer = lax.ppermute(w_part, "tensor", swap)
    keys, begun, carry = remain(*shared, keys, head)
    begun, total = lax.optimization_barrier((begun, near + far))
    far, near = exchange(total, rounds - 1)
    remaining, part = finish(begun, *shared, carry, cotangent, key_weight, total)
    remaining, near, far = lax.optimization_barrier((remaining, near, far))
    new_update, pooled, input_grad = update(lt, sec, near, far, part, w_peer, replicas, m.shape)
    return (keys, input_grad, remaining[None], new_update, pooled.transpose(0, 2, 1))


def solution(mesh):
    placed = (
        P(("groups", "replica"), "tensor"),
        P(("groups", "replica"), "tensor"),
        P("tensor", None),
        P(("groups", "replica"), "tensor", None),
        P("tensor", None, None),
    )
    return jax.shard_map(
        shards,
        mesh=mesh,
        in_specs=placed,
        out_specs=(
            P(("groups", "replica"), "tensor"),
            P(("groups", "replica"), "tensor"),
            P(("groups", "replica"), "tensor", None),
            P(("groups", "tensor"), None),
            P(("groups", "tensor"), None, None),
        ),
        check_vma=False,
    )
```
